32 devices in a mesh: prow: 4 (over y, core), pcol: 8 (over z, x).
Axes of the slice: x: 2, y: 2, z: 4, core: 2. Of those that a mesh axis runs over, the one named last changes fastest.
Arguments:
- coords: float32 [2, 8, 2048], P(None, None, 'prow'), may hold values from 0 to 1
- observations: float32 [8, 2048], P(None, 'prow'), may hold values from -6 to 6
- length_scale: float32 [1], replicated, may hold values from 0.06 to 0.15
- nugget: float32 [1], replicated, may hold values from 0.3 to 1
Outputs:
- slab: float32 [8, 2048, 1024], P(None, 'prow', 'pcol')
- whitened: float32 [8, 2048], P(None, 'prow')
- loglik_part: float32 [1], replicated
The draws below stay inside these ranges and needn't reach their ends.
All inputs are finite; a program needn't handle non-finite values.
Results may differ from the reference program's by a relative error of at most 0.0003.
Values sent between devices are 32-bit elements; how exact they have to be, the bound alone decides.
No kernel may reach another device: no remote copies, remote signals or barrier semaphores. Data moves between devices by JAX's collectives and lax.ppermute only.
A program may use at most 128 MiB of HBM per device.

```python
import math
import jax
import jax.numpy as jnp
from jax import lax

B = 512
RT_DEV = 8
SLAB = 1024
N_PROW = 4


def shard_levels(rng, shape, pieces, low, high):
    def one(dim, blocks):
        steps = jax.random.uniform(jax.random.fold_in(jax.random.fold_in(rng, 6), dim), (blocks,), jnp.float32, low / len(pieces), high / len(pieces))
        return jnp.repeat(jnp.exp(steps), shape[dim] // blocks).reshape((-1,) + (1,) * (len(shape) - dim - 1))

    level = one(*pieces[0])
    for cut in pieces[1:]:
        level = level * one(*cut)
    return level


def centred(key, dims, width, reach, split=(), kind=jnp.bfloat16):
    array = width * jax.random.normal(key, dims, jnp.float32)
    if split:
        array = array * shard_levels(key, dims, split, -0.22, 0.18)
    return jnp.clip(array, -reach, reach).astype(kind)


def setup_inputs(seed: int = 0) -> dict:
    seeds = jax.random.split(jax.random.key(seed), 5)
    return {
        "coords": jnp.clip(1.0 * jax.random.uniform(seeds[0], (2, RT_DEV, N_PROW * B), jnp.float32) ** shard_levels(seeds[0], (2, RT_DEV, N_PROW * B), ((2, 4),), -0.2, 0.2), 0.0, 1.0),
        "observations": centred(seeds[1], (RT_DEV, N_PROW * B), 1.0, 6.0, ((1, 4),), jnp.float32),
        "length_scale": jnp.clip(jax.random.uniform(seeds[2], (1,), jnp.float32, 0.06, 0.15), 0.06, 0.15),
        "nugget": jnp.clip(jax.random.uniform(seeds[3], (1,), jnp.float32, 0.3, 1.0), 0.3, 1.0),
    }


def matern_block(left_x, left_y, right_x, right_y, decay_rate):
    delta_x = left_x[:, None] - right_x[None, :]
    delta_y = left_y[:, None] - right_y[None, :]
    scaled = decay_rate * jnp.sqrt(delta_x * delta_x + delta_y * delta_y)
    return (1.0 + scaled) * jnp.exp(-scaled)

def transposed_product(left, right):
    return jnp.dot(left.astype(jnp.float32), right.T.astype(jnp.float32), precision=lax.Precision.HIGHEST, preferred_element_type=jnp.float32)

def reference(coords, observations, length_scale, nugget):
    flat_x = coords[0].reshape(-1)
    flat_y = coords[1].reshape(-1)
    values = observations.reshape(-1)
    count = flat_x.shape[0]
    decay_rate = math.sqrt(3.0) / length_scale[0]
    nugget_value = nugget[0]
    site_ids = jnp.arange(count, dtype=jnp.int32)

    def covariance(row_lo, row_hi, col_lo, col_hi):
        rows = site_ids[row_lo:row_hi]
        cols = site_ids[col_lo:col_hi]
        same = (rows[:, None] == cols[None, :]).astype(jnp.float32)
        return matern_block(flat_x[row_lo:row_hi], flat_y[row_lo:row_hi], flat_x[col_lo:col_hi], flat_y[col_lo:col_hi], decay_rate) + nugget_value * same
    identity = jnp.eye(B, dtype=jnp.float32)
    cov_first = covariance(0, count, 0, B)
    factor_first = jnp.linalg.cholesky(cov_first[:B])
    inverse_first = jax.scipy.linalg.solve_triangular(factor_first, identity, lower=True)
    panel_first = transposed_product(cov_first, inverse_first)
    panel_first = panel_first.at[:B].set(factor_first)
    cov_second = covariance(0, count, B, 2 * B)
    schur_second = cov_second - transposed_product(panel_first, panel_first[B:2 * B])
    factor_second = jnp.linalg.cholesky(schur_second[B:2 * B])
    inverse_second = jax.scipy.linalg.solve_triangular(factor_second, identity, lower=True)
    panel_second = transposed_product(schur_second, inverse_second)
    panel_second = panel_second.at[:B].set(0.0).at[B:2 * B].set(factor_second)
    slab_lo = 2 * B
    slab_hi = 2 * B + SLAB
    cov_slab = covariance(0, count, slab_lo, slab_hi)
    slab = cov_slab - transposed_product(panel_first, panel_first[slab_lo:slab_hi]) - transposed_product(panel_second, panel_second[slab_lo:slab_hi])
    slab = jnp.where((site_ids < 2 * B)[:, None], 0.0, slab)
    hp = lax.Precision.HIGHEST
    whitened_first = jnp.dot(inverse_first, values[:B], precision=hp)
    whitened_second = jnp.dot(inverse_second, values[B:2 * B] - jnp.dot(panel_first[B:2 * B], whitened_first, precision=hp), precision=hp)
    whitened = values - jnp.dot(panel_first, whitened_first, precision=hp) - jnp.dot(panel_second, whitened_second, precision=hp)
    whitened = whitened.at[:B].set(whitened_first).at[B:2 * B].set(whitened_second)
    quadratic = 0.5 * (jnp.sum(whitened_first * whitened_first) + jnp.sum(whitened_second * whitened_second))
    log_terms = jnp.sum(jnp.log(jnp.diagonal(factor_first))) + jnp.sum(jnp.log(jnp.diagonal(factor_second)))
    loglik_part = -(quadratic + log_terms) / (2.0 * B)
    return (slab.reshape(RT_DEV, N_PROW * B, SLAB), whitened.reshape(RT_DEV, N_PROW * B), loglik_part.reshape(1))
```

```python
import functools

import jax
import jax.numpy as jnp
from jax import lax
from jax.experimental import pallas as pl
from jax.experimental.pallas import tpu as pltpu
from jax.sharding import PartitionSpec as P

SLAB_DEV = 128
NB = 128
SUB = 8


def lane_bcast(v, c):
    return jnp.broadcast_to(v[:, c : c + 1], v.shape)


def row_bcast(v, k):
    return jnp.broadcast_to(v[k : k + 1, :], v.shape)


def split2(x):
    hi = x.astype(jnp.bfloat16)
    lo = (x - hi.astype(jnp.float32)).astype(jnp.bfloat16)
    return hi, lo


def dot_f32(a, b):
    return jnp.dot(a, b, preferred_element_type=jnp.float32)


def dot3(a, b):
    ah, al = split2(a)
    bh, bl = split2(b)
    return dot_f32(ah, bh) + (dot_f32(ah, bl) + dot_f32(al, bh))


def matern(dx, dy, rate2):
    t = (dx * dx + dy * dy) * rate2
    s = t * lax.rsqrt(jnp.maximum(t, 1e-30))
    return (1.0 + s) * jnp.exp(-s)


def tree_sum(xs):
    while len(xs) > 1:
        xs = [xs[i] + xs[i + 1] if i + 1 < len(xs) else xs[i] for i in range(0, len(xs), 2)]
    return xs[0]


def factor_block(rows):
    sub = lax.broadcasted_iota(jnp.int32, (SUB, NB), 0)
    lane = lax.broadcasted_iota(jnp.int32, (SUB, NB), 1)
    units = [(sub == k).astype(jnp.float32) for k in range(SUB)]
    groups = len(rows)
    r_all = list(rows)
    w_all = [(lane == sub + SUB * t).astype(jnp.float32) for t in range(groups)]
    out = []
    logs = jnp.zeros((SUB, NB), jnp.float32)
    for s in range(groups):
        r, w = r_all[s], w_all[s]
        cols = [lane_bcast(r, SUB * s + k) for k in range(SUB)]
        w_out = jnp.zeros((SUB, NB), jnp.float32)
        prod = None
        for k in range(SUB):
            d = row_bcast(cols[k], k)
            inv = 1.0 / d
            rs = lax.rsqrt(d)
            prod = d if prod is None else prod * d
            f = cols[k] - units[k]
            for m in range(k + 1, SUB):
                cols[m] = cols[m] - (f * row_bcast(cols[m], k)) * inv
            wk = row_bcast(w, k)
            w_out = jnp.where(sub == k, wk * rs, w_out)
            r = r - (f * row_bcast(r, k)) * inv
            w = w - (f * wk) * inv
        logs = logs + jnp.log(prod)
        out.append(w_out)
        if s + 1 < groups:
            r_rows = [row_bcast(r, k) for k in range(SUB)]
            w_rows = [row_bcast(w, k) for k in range(SUB)]
            for t in range(s + 1, groups):
                g = [lane_bcast(r_all[t], SUB * s + k) for k in range(SUB)]
                r_all[t] = r_all[t] - tree_sum([g[k] * r_rows[k] for k in range(SUB)])
                w_all[t] = w_all[t] - tree_sum([g[k] * w_rows[k] for k in range(SUB)])
    return out, logs


def kernel(
    tile, ls_ref, ng_ref, lead_ref, loc_ref, obs_ref,
    slab_ref, white_ref, ll_ref,
    a_ref, w_ref, y_ref, site_ref, row_ref, chi_ref, clo_ref, p1_ref, p2_ref, p3_ref,
):
    f32 = jnp.float32
    n_lead = 2 * tile
    nblk = n_lead // NB
    rows_total = loc_ref.shape[1]
    row_rank = lax.axis_index("prow")
    col_rank = lax.axis_index("pcol")
    row_procs = lax.axis_size("prow")
    ls = jnp.full((SUB, NB), ls_ref[0], f32)
    rate2 = 3.0 / (ls * ls)
    nugget = ng_ref[0]
    col_off = col_rank * SLAB_DEV
    col_tile = 2 + col_off // tile
    col_lane = pl.multiple_of(lax.rem(col_off, tile), SLAB_DEV)
    cx = lead_ref[col_tile, 0:1, pl.ds(col_lane, SLAB_DEV)]
    cy = lead_ref[col_tile, 1:2, pl.ds(col_lane, SLAB_DEV)]
    sub = lax.broadcasted_iota(jnp.int32, (SUB, NB), 0)
    lane = lax.broadcasted_iota(jnp.int32, (SUB, NB), 1)

    for q in range(nblk):
        t, o = divmod(q * NB, tile)
        stacked = jnp.concatenate(
            [lead_ref[t, :, o : o + NB], jnp.zeros((NB - 3, NB), f32)], axis=0
        )
        site_ref[q * NB : (q + 1) * NB, :] = stacked.T

    def row_columns(q, c):
        o = pl.multiple_of(q * NB, NB)
        stacked = jnp.concatenate(
            [loc_ref[:, pl.ds(o, NB)], jnp.zeros((NB - 2, NB), f32)], axis=0
        )
        row_ref[pl.ds(o, NB), :] = stacked.T
        return c

    lax.fori_loop(0, rows_total // NB, row_columns, 0)

    for b in range(nblk):
        def cov_rows(g, c, b=b):
            o = pl.multiple_of(b * NB + g * SUB, SUB)
            v = site_ref[pl.ds(o, SUB), :]
            x, y, ob = lane_bcast(v, 0), lane_bcast(v, 1), lane_bcast(v, 2)
            for j in range(b, nblk):
                t, u = divmod(j * NB, tile)
                val = matern(
                    x - lead_ref[t, 0:1, u : u + NB], y - lead_ref[t, 1:2, u : u + NB], rate2
                )
                if j == b:
                    val = jnp.where(lane == sub + g * SUB, val + nugget, val)
                a_ref[pl.ds(o, SUB), j * NB : (j + 1) * NB] = val
            a_ref[pl.ds(o, SUB), n_lead : n_lead + NB] = matern(x - cx, y - cy, rate2)
            a_ref[pl.ds(o, SUB), n_lead + NB : n_lead + 2 * NB] = jnp.where(lane < 2, ob, 0.0)
            return c

        lax.fori_loop(0, NB // SUB, cov_rows, 0)

    chunk = rows_total // nblk
    width = n_lead + 2 * NB

    def step(b, logs):
        o = pl.multiple_of(b * NB, NB)
        rows = [
            a_ref[pl.ds(pl.multiple_of(b * NB + SUB * t, SUB), SUB), pl.ds(o, NB)]
            for t in range(NB // SUB)
        ]
        out, more = factor_block(rows)
        w = jnp.concatenate(out, axis=0)
        w_ref[pl.ds(o, NB), :] = w

        def cov_chunk(g, c):
            ro = pl.multiple_of(b * chunk + g * 16, 16)
            for j in range(nblk):
                t, u = divmod(j * NB, tile)
                vals = []
                for h in range(2):
                    v = row_ref[pl.ds(pl.multiple_of(ro + h * SUB, SUB), SUB), :]
                    vals.append(matern(
                        lane_bcast(v, 0) - lead_ref[t, 0:1, u : u + NB],
                        lane_bcast(v, 1) - lead_ref[t, 1:2, u : u + NB],
                        rate2,
                    ))
                hi, lo = split2(jnp.concatenate(vals, axis=0))
                chi_ref[pl.ds(ro, 16), j * NB : (j + 1) * NB] = hi
                clo_ref[pl.ds(ro, 16), j * NB : (j + 1) * NB] = lo
            return c

        lax.fori_loop(0, chunk // 16, cov_chunk, 0)

        for bb in range(nblk):
            @pl.when(b == bb)
            def _(bb=bb):
                r0, c0 = bb * NB, (bb + 1) * NB
                u = dot3(w, a_ref[r0 : r0 + NB, c0:width])
                a_ref[r0 : r0 + NB, c0:width] = u
                uh, ul = split2(u)
                for t in range(bb + 1, nblk):
                    lo = t * NB - c0
                    th = uh[:, lo : lo + NB].T
                    tl = ul[:, lo : lo + NB].T
                    rh, rl = uh[:, lo:], ul[:, lo:]
                    p = dot_f32(th, rh) + (dot_f32(th, rl) + dot_f32(tl, rh))
                    a_ref[t * NB : (t + 1) * NB, t * NB : width] -= p
        return logs + more

    logs = lax.fori_loop(0, nblk, step, jnp.zeros((SUB, NB), f32))

    for b in reversed(range(nblk)):
        r0, c0 = b * NB, (b + 1) * NB
        v = a_ref[r0:c0, n_lead:width]
        if b + 1 < nblk:
            v = v - dot3(a_ref[r0:c0, c0:n_lead], y_ref[c0:n_lead, :])
        y_ref[r0:c0, :] = dot3(w_ref[r0:c0, :].T, v)

    y = y_ref[...]
    yh, yl = split2(y)
    yt = ((y - yh.astype(f32)) - yl.astype(f32)).astype(jnp.bfloat16)
    first = lax.broadcasted_iota(jnp.int32, (n_lead, NB), 1) == 0
    p1_ref[...] = jnp.concatenate([yh[:, :NB], yl[:, :NB]], axis=1)
    obs_h, obs_l = yh[:, NB:].astype(f32), yl[:, NB:].astype(f32)
    p2_ref[...] = jnp.concatenate(
        [yt[:, :NB], jnp.where(first, obs_h, obs_l).astype(jnp.bfloat16)], axis=1
    )
    p3_ref[...] = jnp.concatenate(
        [yh[:, :NB], jnp.where(first, obs_h, 0.0).astype(jnp.bfloat16)], axis=1
    )

    z = a_ref[:, n_lead + NB : width]
    quad = 0.5 * jnp.sum(jnp.where(lax.broadcasted_iota(jnp.int32, z.shape, 1) == 0, z * z, 0.0), keepdims=True)
    ll_ref[...] = -(quad + 0.5 * logs[0:1, 0:1]) / float(n_lead)

    big = 2 * NB
    per_tile = tile // big

    for q in range(rows_total // big):
        o = q * big
        ch = chi_ref[o : o + big, :]
        acc = dot_f32(ch, p1_ref[...])
        acc2 = dot_f32(ch, p2_ref[...]) + dot_f32(clo_ref[o : o + big, :], p3_ref[...])
        corr = acc[:, :NB] + (acc[:, NB:] + acc2[:, :NB])
        t, off = divmod(o, tile)
        gid = (t * row_procs + row_rank) * tile + off
        leading = gid < n_lead
        v = row_ref[o : o + big, :]
        x = jnp.broadcast_to(v[:, 0:1], (big, NB))
        y = jnp.broadcast_to(v[:, 1:2], (big, NB))
        val = matern(x - cx, y - cy, rate2[0:1, :])
        rid = gid + lax.broadcasted_iota(jnp.int32, (big, NB), 0)
        cid = n_lead + col_off + lax.broadcasted_iota(jnp.int32, (big, NB), 1)
        val = jnp.where(rid == cid, val + nugget, val) - corr
        slab_ref[o : o + big, :] = jnp.where(leading, 0.0, val)
        for h in range(2):
            at = off + h * NB
            tr = acc2[h * NB : (h + 1) * NB, NB:].T
            rest = obs_ref[t : t + 1, at : at + NB] - (tr[0:1, :] + tr[1:2, :])
            if t == 0:
                zs = pl.multiple_of(jnp.where(leading, gid, 0) + h * NB, NB)
                zt = a_ref[pl.ds(zs, NB), n_lead + NB : width].T
                rest = jnp.where(leading, zt[0:1, :], rest)
            white_ref[t : t + 1, at : at + NB] = rest


def shards(coords, observations, length_scale, nugget):
    tile_count, tile = coords.shape[1:]
    rows = tile_count * tile
    n_lead = 2 * tile
    f32, bf16 = jnp.float32, jnp.bfloat16
    mine = jnp.concatenate([coords[:, 0, :], observations[0:1, :]], axis=0)
    lead = lax.all_gather(mine, "prow", axis=0)
    vmem = pl.BlockSpec(memory_space=pltpu.VMEM)
    smem = pl.BlockSpec(memory_space=pltpu.SMEM)
    slab, white, ll = pl.pallas_call(
        functools.partial(kernel, tile),
        out_shape=(
            jax.ShapeDtypeStruct((rows, SLAB_DEV), f32),
            jax.ShapeDtypeStruct((tile_count, tile), f32),
            jax.ShapeDtypeStruct((1, 1), f32),
        ),
        in_specs=[smem, smem, vmem, vmem, vmem],
        out_specs=(vmem, vmem, vmem),
        scratch_shapes=[
            pltpu.VMEM((n_lead, n_lead + 2 * NB), f32),
            pltpu.VMEM((n_lead, NB), f32),
            pltpu.VMEM((n_lead, 2 * NB), f32),
            pltpu.VMEM((n_lead, NB), f32),
            pltpu.VMEM((rows, NB), f32),
            pltpu.VMEM((rows, n_lead), bf16),
            pltpu.VMEM((rows, n_lead), bf16),
            pltpu.VMEM((n_lead, 2 * NB), bf16),
            pltpu.VMEM((n_lead, 2 * NB), bf16),
            pltpu.VMEM((n_lead, 2 * NB), bf16),
        ],
        compiler_params=pltpu.CompilerParams(vmem_limit_bytes=48 * 1024 * 1024),
    )(length_scale, nugget, lead, coords.reshape(2, rows), observations)
    return slab.reshape(tile_count, tile, SLAB_DEV), white, ll.reshape(1)


def solution(mesh):
    placed = (P(None, None, "prow"), P(None, "prow"), P(), P())
    return jax.shard_map(
        shards,
        mesh=mesh,
        in_specs=placed,
        out_specs=(P(None, "prow", "pcol"), P(None, "prow"), P()),
        check_vma=False,
    )
```

```python
import functools

import jax
import jax.numpy as jnp
from jax import lax
from jax.experimental import pallas as pl
from jax.experimental.pallas import tpu as pltpu
from jax.sharding import PartitionSpec as P

SLAB_DEV = 128
NB = 128
SUB = 8


def lane_bcast(v, c):
    return jnp.broadcast_to(v[:, c : c + 1], v.shape)


def row_bcast(v, k):
    return jnp.broadcast_to(v[k : k + 1, :], v.shape)


def split2(x):
    hi = x.astype(jnp.bfloat16)
    lo = (x - hi.astype(jnp.float32)).astype(jnp.bfloat16)
    return hi, lo


def dot_f32(a, b):
    return jnp.dot(a, b, preferred_element_type=jnp.float32)


def dot3(a, b):
    ah, al = split2(a)
    bh, bl = split2(b)
    return dot_f32(ah, bh) + (dot_f32(ah, bl) + dot_f32(al, bh))


LOG2E = 1.4426950408889634


def matern(dx, dy, rate2):
    t = (dx * dx + dy * dy) * rate2
    s = t * lax.rsqrt(jnp.maximum(t, 1e-30))
    e = jnp.exp2(s * -LOG2E)
    return e + s * e


def tree_sum(xs):
    while len(xs) > 1:
        xs = [xs[i] + xs[i + 1] if i + 1 < len(xs) else xs[i] for i in range(0, len(xs), 2)]
    return xs[0]


def factor_block(rows, fill):
    sub = lax.broadcasted_iota(jnp.int32, (SUB, NB), 0)
    lane = lax.broadcasted_iota(jnp.int32, (SUB, NB), 1)
    units = [(sub == k).astype(jnp.float32) for k in range(SUB)]
    groups = len(rows)
    r_all = list(rows)
    w_all = [(lane == sub + SUB * t).astype(jnp.float32) for t in range(groups)]
    out = []
    logs = jnp.zeros((SUB, NB), jnp.float32)
    cols = [lane_bcast(r_all[0], k) for k in range(SUB)]
    for s in range(groups):
        r, w = r_all[s], w_all[s]
        more = s + 1 < groups
        if more:
            g_next = [lane_bcast(r_all[s + 1], SUB * s + k) for k in range(SUB)]
            low = list(g_next)
            ahead = [lane_bcast(r_all[s + 1], SUB * (s + 1) + k) for k in range(SUB)]
        w_out = jnp.zeros((SUB, NB), jnp.float32)
        prod = None
        for k in range(SUB):
            d = row_bcast(cols[k], k)
            inv = pltpu.reciprocal(d, approx=True)
            rs = lax.rsqrt(d)
            prod = d if prod is None else prod * d
            f = cols[k] - units[k]
            for m in range(k + 1, SUB):
                e = row_bcast(cols[m], k)
                cols[m] = cols[m] - (f * e) * inv
                if more:
                    low[m] = low[m] - low[k] * (e * inv)
            if more:
                h = low[k] * inv
                for m in range(SUB):
                    ahead[m] = ahead[m] - h * row_bcast(low[k], m)
            wk = row_bcast(w, k)
            w_out = jnp.where(sub == k, wk * rs, w_out)
            r = r - (f * row_bcast(r, k)) * inv
            w = w - (f * wk) * inv
            fill(s, k)
        logs = logs + jnp.log(prod)
        out.append(w_out)
        if more:
            r_rows = [row_bcast(r, k) for k in range(SUB)]
            w_rows = [row_bcast(w, k) for k in range(SUB)]
            for t in range(s + 1, groups):
                g = g_next if t == s + 1 else [
                    lane_bcast(r_all[t], SUB * s + k) for k in range(SUB)
                ]
                r_all[t] = r_all[t] - tree_sum([g[k] * r_rows[k] for k in range(SUB)])
                w_all[t] = w_all[t] - tree_sum([g[k] * w_rows[k] for k in range(SUB)])
            cols = ahead
    return out, logs


def kernel(
    tile, ls_ref, ng_ref, lead_ref, loc_ref, obs_ref,
    slab_ref, white_ref, ll_ref,
    a_ref, w_ref, y_ref, site_ref, row_ref, chi_ref, clo_ref, p1_ref, p2_ref, p3_ref,
):
    f32 = jnp.float32
    n_lead = 2 * tile
    nblk = n_lead // NB
    rows_total = loc_ref.shape[1]
    row_rank = lax.axis_index("prow")
    col_rank = lax.axis_index("pcol")
    row_procs = lax.axis_size("prow")
    ls = jnp.full((SUB, NB), ls_ref[0], f32)
    rate2 = 3.0 / (ls * ls)
    nugget = ng_ref[0]
    col_off = col_rank * SLAB_DEV
    col_tile = 2 + col_off // tile
    col_lane = pl.multiple_of(lax.rem(col_off, tile), SLAB_DEV)
    cx = lead_ref[col_tile, 0:1, pl.ds(col_lane, SLAB_DEV)]
    cy = lead_ref[col_tile, 1:2, pl.ds(col_lane, SLAB_DEV)]
    sub = lax.broadcasted_iota(jnp.int32, (SUB, NB), 0)
    lane = lax.broadcasted_iota(jnp.int32, (SUB, NB), 1)

    for q in range(nblk):
        t, o = divmod(q * NB, tile)
        stacked = jnp.concatenate(
            [lead_ref[t, :, o : o + NB], jnp.zeros((NB - 3, NB), f32)], axis=0
        )
        site_ref[q * NB : (q + 1) * NB, :] = stacked.T

    for b in range(nblk):
        def cov_rows(g, c, b=b):
            o = pl.multiple_of(b * NB + g * SUB, SUB)
            v = site_ref[pl.ds(o, SUB), :]
            x, y, ob = lane_bcast(v, 0), lane_bcast(v, 1), lane_bcast(v, 2)
            for j in range(b, nblk):
                t, u = divmod(j * NB, tile)
                val = matern(
                    x - lead_ref[t, 0:1, u : u + NB], y - lead_ref[t, 1:2, u : u + NB], rate2
                )
                if j == b:
                    val = jnp.where(lane == sub + g * SUB, val + nugget, val)
                a_ref[pl.ds(o, SUB), j * NB : (j + 1) * NB] = val
            a_ref[pl.ds(o, SUB), n_lead : n_lead + NB] = matern(x - cx, y - cy, rate2)
            a_ref[pl.ds(o, SUB), n_lead + NB : n_lead + 2 * NB] = jnp.where(lane < 2, ob, 0.0)
            return c

        lax.fori_loop(0, NB // SUB, cov_rows, 0, unroll=4)

    chunk = rows_total // nblk
    width = n_lead + 2 * NB

    def step(b, logs):
        o = pl.multiple_of(b * NB, NB)
        rows = [
            a_ref[pl.ds(pl.multiple_of(b * NB + SUB * t, SUB), SUB), pl.ds(o, NB)]
            for t in range(NB // SUB)
        ]
        for q in range(chunk // NB):
            at = pl.multiple_of(b * chunk + q * NB, NB)
            stacked = jnp.concatenate(
                [loc_ref[:, pl.ds(at, NB)], jnp.zeros((NB - 2, NB), f32)], axis=0
            )
            row_ref[pl.ds(at, NB), :] = stacked.T

        per_group = chunk // (NB // SUB)
        units_total = (per_group // 16) * nblk
        held = {}

        def fill(s, k):
            for unit in range(k * units_total // SUB, (k + 1) * units_total // SUB):
                pair, j = divmod(unit, nblk)
                ro = pl.multiple_of(b * chunk + s * per_group + pair * 16, 16)
                if j == 0:
                    for h in range(2):
                        v = row_ref[pl.ds(pl.multiple_of(ro + h * SUB, SUB), SUB), :]
                        held[h] = lane_bcast(v, 0), lane_bcast(v, 1)
                t, u = divmod(j * NB, tile)
                vals = [
                    matern(
                        held[h][0] - lead_ref[t, 0:1, u : u + NB],
                        held[h][1] - lead_ref[t, 1:2, u : u + NB],
                        rate2,
                    )
                    for h in range(2)
                ]
                hi, lo = split2(jnp.concatenate(vals, axis=0))
                chi_ref[pl.ds(ro, 16), j * NB : (j + 1) * NB] = hi
                clo_ref[pl.ds(ro, 16), j * NB : (j + 1) * NB] = lo

        out, more = factor_block(rows, fill)
        w = jnp.concatenate(out, axis=0)
        w_ref[pl.ds(o, NB), :] = w

        for bb in range(nblk):
            @pl.when(b == bb)
            def _(bb=bb):
                r0, c0 = bb * NB, (bb + 1) * NB
                u = dot3(w, a_ref[r0 : r0 + NB, c0:width])
                a_ref[r0 : r0 + NB, c0:width] = u
                uh, ul = split2(u)
                for t in range(bb + 1, nblk):
                    lo = t * NB - c0
                    th = uh[:, lo : lo + NB].T
                    tl = ul[:, lo : lo + NB].T
                    rh, rl = uh[:, lo:], ul[:, lo:]
                    p = dot_f32(th, rh) + (dot_f32(th, rl) + dot_f32(tl, rh))
                    a_ref[t * NB : (t + 1) * NB, t * NB : width] -= p
        return logs + more

    logs = lax.fori_loop(0, nblk, step, jnp.zeros((SUB, NB), f32))

    for b in reversed(range(nblk)):
        r0, c0 = b * NB, (b + 1) * NB
        v = a_ref[r0:c0, n_lead:width]
        if b + 1 < nblk:
            v = v - dot3(a_ref[r0:c0, c0:n_lead], y_ref[c0:n_lead, :])
        y_ref[r0:c0, :] = dot3(w_ref[r0:c0, :].T, v)

    y = y_ref[...]
    yh, yl = split2(y)
    yt = ((y - yh.astype(f32)) - yl.astype(f32)).astype(jnp.bfloat16)
    first = lax.broadcasted_iota(jnp.int32, (n_lead, NB), 1) == 0
    p1_ref[...] = jnp.concatenate([yh[:, :NB], yl[:, :NB]], axis=1)
    obs_h, obs_l = yh[:, NB:].astype(f32), yl[:, NB:].astype(f32)
    p2_ref[...] = jnp.concatenate(
        [yt[:, :NB], jnp.where(first, obs_h, obs_l).astype(jnp.bfloat16)], axis=1
    )
    p3_ref[...] = jnp.concatenate(
        [yh[:, :NB], jnp.where(first, obs_h, 0.0).astype(jnp.bfloat16)], axis=1
    )

    z = a_ref[:, n_lead + NB : width]
    quad = 0.5 * jnp.sum(jnp.where(lax.broadcasted_iota(jnp.int32, z.shape, 1) == 0, z * z, 0.0), keepdims=True)
    ll_ref[...] = -(quad + 0.5 * logs[0:1, 0:1]) / float(n_lead)

    big = 2 * NB
    per_tile = tile // big

    for q in range(rows_total // big):
        o = q * big
        ch = chi_ref[o : o + big, :]
        acc = dot_f32(ch, p1_ref[...])
        acc2 = dot_f32(ch, p2_ref[...]) + dot_f32(clo_ref[o : o + big, :], p3_ref[...])
        corr = acc[:, :NB] + (acc[:, NB:] + acc2[:, :NB])
        t, off = divmod(o, tile)
        gid = (t * row_procs + row_rank) * tile + off
        leading = gid < n_lead
        v = row_ref[o : o + big, :]
        x = jnp.broadcast_to(v[:, 0:1], (big, NB))
        y = jnp.broadcast_to(v[:, 1:2], (big, NB))
        val = matern(x - cx, y - cy, rate2[0:1, :])
        rid = gid + lax.broadcasted_iota(jnp.int32, (big, NB), 0)
        cid = n_lead + col_off + lax.broadcasted_iota(jnp.int32, (big, NB), 1)
        val = jnp.where(rid == cid, val + nugget, val) - corr
        slab_ref[o : o + big, :] = jnp.where(leading, 0.0, val)
        for h in range(2):
            at = off + h * NB
            tr = acc2[h * NB : (h + 1) * NB, NB:].T
            rest = obs_ref[t : t + 1, at : at + NB] - (tr[0:1, :] + tr[1:2, :])
            if t == 0:
                zs = pl.multiple_of(jnp.where(leading, gid, 0) + h * NB, NB)
                zt = a_ref[pl.ds(zs, NB), n_lead + NB : width].T
                rest = jnp.where(leading, zt[0:1, :], rest)
            white_ref[t : t + 1, at : at + NB] = rest


def shards(coords, observations, length_scale, nugget):
    tile_count, tile = coords.shape[1:]
    rows = tile_count * tile
    n_lead = 2 * tile
    f32, bf16 = jnp.float32, jnp.bfloat16
    mine = jnp.concatenate([coords[:, 0, :], observations[0:1, :]], axis=0)
    lead = lax.all_gather(mine, "prow", axis=0)
    vmem = pl.BlockSpec(memory_space=pltpu.VMEM)
    smem = pl.BlockSpec(memory_space=pltpu.SMEM)
    slab, white, ll = pl.pallas_call(
        functools.partial(kernel, tile),
        out_shape=(
            jax.ShapeDtypeStruct((rows, SLAB_DEV), f32),
            jax.ShapeDtypeStruct((tile_count, tile), f32),
            jax.ShapeDtypeStruct((1, 1), f32),
        ),
        in_specs=[smem, smem, vmem, vmem, vmem],
        out_specs=(vmem, vmem, vmem),
        scratch_shapes=[
            pltpu.VMEM((n_lead, n_lead + 2 * NB), f32),
            pltpu.VMEM((n_lead, NB), f32),
            pltpu.VMEM((n_lead, 2 * NB), f32),
            pltpu.VMEM((n_lead, NB), f32),
            pltpu.VMEM((rows, NB), f32),
            pltpu.VMEM((rows, n_lead), bf16),
            pltpu.VMEM((rows, n_lead), bf16),
            pltpu.VMEM((n_lead, 2 * NB), bf16),
            pltpu.VMEM((n_lead, 2 * NB), bf16),
            pltpu.VMEM((n_lead, 2 * NB), bf16),
        ],
        compiler_params=pltpu.CompilerParams(vmem_limit_bytes=48 * 1024 * 1024),
    )(length_scale, nugget, lead, coords.reshape(2, rows), observations)
    return slab.reshape(tile_count, tile, SLAB_DEV), white, ll.reshape(1)


def solution(mesh):
    placed = (P(None, None, "prow"), P(None, "prow"), P(), P())
    return jax.shard_map(
        shards,
        mesh=mesh,
        in_specs=placed,
        out_specs=(P(None, "prow", "pcol"), P(None, "prow"), P()),
        check_vma=False,
    )
```

```python
import functools

import jax
import jax.numpy as jnp
from jax import lax
from jax.experimental import pallas as pl
from jax.experimental.pallas import tpu as pltpu
from jax.sharding import PartitionSpec as P

SLAB_DEV = 128
NB = 128
SUB = 8


def lane_bcast(v, c):
    return jnp.broadcast_to(v[:, c : c + 1], v.shape)


def row_bcast(v, k):
    return jnp.broadcast_to(v[k : k + 1, :], v.shape)


def split2(x):
    hi = x.astype(jnp.bfloat16)
    lo = (x - hi.astype(jnp.float32)).astype(jnp.bfloat16)
    return hi, lo


def dot_f32(a, b):
    return jnp.dot(a, b, preferred_element_type=jnp.float32)


LOG2E = 1.4426950408889634


def matern(dx, dy, rate2):
    t = (dx * dx + dy * dy) * rate2
    s = t * lax.rsqrt(jnp.maximum(t, 1e-30))
    e = jnp.exp2(s * -LOG2E)
    return e + s * e


def tree_sum(xs):
    while len(xs) > 1:
        xs = [xs[i] + xs[i + 1] if i + 1 < len(xs) else xs[i] for i in range(0, len(xs), 2)]
    return xs[0]


def factor_block(rows, fill):
    sub = lax.broadcasted_iota(jnp.int32, (SUB, NB), 0)
    lane = lax.broadcasted_iota(jnp.int32, (SUB, NB), 1)
    units = [(sub == k).astype(jnp.float32) for k in range(SUB)]
    groups = len(rows)
    r_all = list(rows)
    w_all = [(lane == sub + SUB * t).astype(jnp.float32) for t in range(groups)]
    out = []
    logs = jnp.zeros((SUB, NB), jnp.float32)
    cols = [lane_bcast(r_all[0], k) for k in range(SUB)]
    for s in range(groups):
        r, w = r_all[s], w_all[s]
        more = s + 1 < groups
        if more:
            g_next = [lane_bcast(r_all[s + 1], SUB * s + k) for k in range(SUB)]
            low = list(g_next)
            ahead = [lane_bcast(r_all[s + 1], SUB * (s + 1) + k) for k in range(SUB)]
        w_out = jnp.zeros((SUB, NB), jnp.float32)
        prod = None
        for k in range(SUB):
            d = row_bcast(cols[k], k)
            inv = pltpu.reciprocal(d, approx=True)
            rs = lax.rsqrt(d)
            prod = d if prod is None else prod * d
            f = cols[k] - units[k]
            fi = f * inv
            h = low[k] * inv if more else None
            for m in range(k + 1, SUB):
                e = row_bcast(cols[m], k)
                cols[m] = cols[m] - ((f * e) * inv if m == k + 1 else fi * e)
                if more:
                    low[m] = low[m] - h * e
            if more:
                for m in range(SUB):
                    ahead[m] = ahead[m] - h * row_bcast(low[k], m)
            wk = row_bcast(w, k)
            w_out = jnp.where(sub == k, wk * rs, w_out)
            r = r - fi * row_bcast(r, k)
            w = w - fi * wk
            fill(s, k)
        logs = logs + jnp.log(prod)
        out.append(w_out)
        if more:
            r_rows = [row_bcast(r, k) for k in range(SUB)]
            w_rows = [row_bcast(w, k) for k in range(SUB)]
            for t in range(s + 1, groups):
                g = g_next if t == s + 1 else [
                    lane_bcast(r_all[t], SUB * s + k) for k in range(SUB)
                ]
                r_all[t] = r_all[t] - tree_sum([g[k] * r_rows[k] for k in range(SUB)])
                w_all[t] = w_all[t] - tree_sum([g[k] * w_rows[k] for k in range(SUB)])
            cols = ahead
    return out, logs


def kernel(
    tile, ls_ref, ng_ref, lead_ref, loc_ref, obs_ref,
    slab_ref, white_ref, ll_ref,
    a_ref, z_ref, site_ref, row_ref, chi_ref, clo_ref, p1_ref, p2_ref, p3_ref,
    d_ref, winv_ref, pinv_ref, col_ref, mh_ref, ml_ref,
):
    f32, bf16 = jnp.float32, jnp.bfloat16
    n_lead = 2 * tile
    nblk = n_lead // NB
    width = n_lead + 2 * NB
    rows_total = loc_ref.shape[1]
    row_rank = lax.axis_index("prow")
    col_rank = lax.axis_index("pcol")
    row_procs = lax.axis_size("prow")
    ls = jnp.full((SUB, NB), ls_ref[0], f32)
    rate2 = 3.0 / (ls * ls)
    nugget = ng_ref[0]
    col_off = col_rank * SLAB_DEV
    col_tile = 2 + col_off // tile
    col_lane = pl.multiple_of(lax.rem(col_off, tile), SLAB_DEV)
    cx = lead_ref[col_tile, 0:1, pl.ds(col_lane, SLAB_DEV)]
    cy = lead_ref[col_tile, 1:2, pl.ds(col_lane, SLAB_DEV)]
    sub = lax.broadcasted_iota(jnp.int32, (SUB, NB), 0)
    lane = lax.broadcasted_iota(jnp.int32, (SUB, NB), 1)

    def columns(coord):
        pad = jnp.zeros((NB - coord.shape[0], NB), f32)
        return jnp.concatenate([coord, pad], axis=0).T

    def site_columns(q):
        t, o = divmod(q * NB, tile)
        site_ref[q * NB : (q + 1) * NB, :] = columns(lead_ref[t, :, o : o + NB])

    def row_columns(q):
        row_ref[q * NB : (q + 1) * NB, :] = columns(loc_ref[:, q * NB : (q + 1) * NB])

    held = {}

    def cov_piece(b, g, j):
        o = b * NB + g * SUB
        if ("site", o) not in held:
            v = site_ref[o : o + SUB, :]
            held["site", o] = [lane_bcast(v, c) for c in range(3)]
        x, y, ob = held["site", o]
        if j < nblk:
            t, u = divmod(j * NB, tile)
            val = matern(x - lead_ref[t, 0:1, u : u + NB], y - lead_ref[t, 1:2, u : u + NB], rate2)
            if j == b:
                val = jnp.where(lane == sub + g * SUB, val + nugget, val)
        elif j == nblk:
            val = matern(x - cx, y - cy, rate2)
        else:
            val = jnp.where(lane < 2, ob, 0.0)
        a_ref[o : o + SUB, j * NB : (j + 1) * NB] = val

    def row_piece(ro, key, j):
        if key not in held:
            held[key] = []
            for h in range(2):
                v = row_ref[pl.ds(pl.multiple_of(ro + h * SUB, SUB), SUB), :]
                held[key].append((lane_bcast(v, 0), lane_bcast(v, 1)))
        t, u = divmod(j * NB, tile)
        vals = [
            matern(x - lead_ref[t, 0:1, u : u + NB], y - lead_ref[t, 1:2, u : u + NB], rate2)
            for x, y in held[key]
        ]
        hi, lo = split2(jnp.concatenate(vals, axis=0))
        chi_ref[pl.ds(ro, 16), j * NB : (j + 1) * NB] = hi
        clo_ref[pl.ds(ro, 16), j * NB : (j + 1) * NB] = lo

    def three(al_parts, bh, bl):
        depth = bh.shape[0]
        return dot_f32(al_parts, jnp.concatenate([bh, bh], axis=0)) + dot_f32(
            al_parts[:, :depth], bl
        )

    def parts(x):
        return jnp.concatenate(split2(x), axis=1)

    def multiplier_piece(j0, j1):
        m = three(pinv_ref[...], *split2(a_ref[0:NB, j0:j1]))
        mh_ref[:, j0:j1], ml_ref[:, j0:j1] = split2(m)
        return m

    def column_parts():
        col_ref[...] = parts(a_ref[NB:n_lead, 0:NB])

    def update_piece(j0, j1, r0, r1, shift):
        new = a_ref[r0:r1, j0:j1] - three(
            col_ref[r0 - NB : r1 - NB, :], mh_ref[:, j0:j1], ml_ref[:, j0:j1]
        )
        a_ref[r0 - NB : r1 - NB, j0 - shift : j1 - shift] = new

    def tile_pieces(j0, j1, shift):
        box = {}

        def first():
            box["m"] = multiplier_piece(j0, j1)

        def last():
            a_ref[n_lead - NB : n_lead, j0 - shift : j1 - shift] = box["m"]

        half = (nblk // 2 + 1) * NB
        return [
            first,
            functools.partial(update_piece, j0, j1, NB, half, shift),
            functools.partial(update_piece, j0, j1, half, n_lead, shift),
            last,
        ]

    def keep_z(at):
        z_ref[pl.ds(at, NB), :] = three(
            winv_ref[...], *split2(a_ref[0:NB, n_lead + NB : width])
        )

    def finish_block(out, more_blocks):
        w = jnp.concatenate(out, axis=0)
        wt = w.T
        w_parts = parts(w)
        winv_ref[...] = w_parts
        wh, wl = w_parts[:, :NB], w_parts[:, NB:]
        if more_blocks:
            u = three(w_parts, *split2(a_ref[0:NB, NB : 2 * NB]))
            ut = three(parts(a_ref[NB : 2 * NB, 0:NB]), *split2(wt))
            d_ref[...] = a_ref[NB : 2 * NB, NB : 2 * NB] - three(parts(ut), *split2(u))
        pinv_ref[...] = parts(three(parts(wt), wh, wl))

    def load_rows():
        return [d_ref[SUB * t : SUB * (t + 1), :] for t in range(NB // SUB)]

    slots = (NB // SUB) * SUB

    def planned(urgent, work):
        plan = [[] for _ in range(slots)]
        early = slots * 7 // 8
        for i, f in enumerate(urgent):
            plan[i * early // len(urgent)].append(f)
        for i, f in enumerate(work):
            plan[i * slots // len(work)].append(f)

        def fill(s, k):
            for f in plan[s * SUB + k]:
                f()

        return fill

    for q in range(nblk):
        site_columns(q)
    for g in range(NB // SUB):
        cov_piece(0, g, 0)
    d_ref[...] = a_ref[0:NB, 0:NB]
    work = [
        functools.partial(cov_piece, b, g, j)
        for b in range(nblk)
        for g in range(NB // SUB)
        for j in range(nblk + 2)
        if (b, j) != (0, 0)
    ]
    urgent = [functools.partial(row_columns, q) for q in range(rows_total // NB)]
    out, logs = factor_block(load_rows(), planned(urgent, work))
    finish_block(out, True)

    chunk = -(-rows_total // 16 // (nblk - 1)) * 16
    col_tiles = [(j * NB, min(j + 2, nblk) * NB) for j in range(1, nblk, 2)]

    def step(b, logs):
        held.clear()
        base = jnp.minimum((b - 1) * chunk, rows_total - chunk)
        work = [
            functools.partial(
                row_piece, pl.multiple_of(base + pair * 16, 16), ("row", pair), j
            )
            for pair in range(chunk // 16)
            for j in range(nblk)
        ]
        urgent = [column_parts]
        for j0, j1 in col_tiles:
            urgent += tile_pieces(j0, j1, NB)
        urgent += [functools.partial(keep_z, pl.multiple_of((b - 1) * NB, NB))]
        urgent += tile_pieces(n_lead, width, 0)
        out, more = factor_block(load_rows(), planned(urgent, work))
        finish_block(out, True)
        return logs + more

    logs = lax.fori_loop(1, nblk, step, logs)
    column_parts()
    keep_z(n_lead - NB)
    for f in tile_pieces(n_lead, width, 0):
        f()

    y = a_ref[:, n_lead:width]
    yh, yl = split2(y)
    yt = ((y - yh.astype(f32)) - yl.astype(f32)).astype(bf16)
    first = lax.broadcasted_iota(jnp.int32, (n_lead, NB), 1) == 0
    p1_ref[...] = jnp.concatenate([yh[:, :NB], yl[:, :NB]], axis=1)
    obs_h, obs_l = yh[:, NB:].astype(f32), yl[:, NB:].astype(f32)
    p2_ref[...] = jnp.concatenate(
        [yt[:, :NB], jnp.where(first, obs_h, obs_l).astype(bf16)], axis=1
    )
    p3_ref[...] = jnp.concatenate(
        [yh[:, :NB], jnp.where(first, obs_h, 0.0).astype(bf16)], axis=1
    )

    z = z_ref[...]
    quad = 0.5 * jnp.sum(jnp.where(first, z * z, 0.0), keepdims=True)
    ll_ref[...] = -(quad + 0.5 * logs[0:1, 0:1]) / float(n_lead)

    big = 2 * NB
    for q in range(rows_total // big):
        o = q * big
        ch = chi_ref[o : o + big, :]
        acc = dot_f32(ch, p1_ref[...])
        acc2 = dot_f32(ch, p2_ref[...]) + dot_f32(clo_ref[o : o + big, :], p3_ref[...])
        corr = acc[:, :NB] + (acc[:, NB:] + acc2[:, :NB])
        t, off = divmod(o, tile)
        gid = (t * row_procs + row_rank) * tile + off
        leading = gid < n_lead
        v = row_ref[o : o + big, :]
        x = jnp.broadcast_to(v[:, 0:1], (big, NB))
        y = jnp.broadcast_to(v[:, 1:2], (big, NB))
        val = matern(x - cx, y - cy, rate2[0:1, :])
        rid = gid + lax.broadcasted_iota(jnp.int32, (big, NB), 0)
        cid = n_lead + col_off + lax.broadcasted_iota(jnp.int32, (big, NB), 1)
        val = jnp.where(rid == cid, val + nugget, val) - corr
        slab_ref[o : o + big, :] = jnp.where(leading, 0.0, val)
        for h in range(2):
            at = off + h * NB
            tr = acc2[h * NB : (h + 1) * NB, NB:].T
            rest = obs_ref[t : t + 1, at : at + NB] - (tr[0:1, :] + tr[1:2, :])
            if t == 0:
                zs = pl.multiple_of(jnp.where(leading, gid, 0) + h * NB, NB)
                zt = z_ref[pl.ds(zs, NB), :].T
                rest = jnp.where(leading, zt[0:1, :], rest)
            white_ref[t : t + 1, at : at + NB] = rest


def shards(coords, observations, length_scale, nugget):
    tile_count, tile = coords.shape[1:]
    rows = tile_count * tile
    n_lead = 2 * tile
    width = n_lead + 2 * NB
    f32, bf16 = jnp.float32, jnp.bfloat16
    mine = jnp.concatenate([coords[:, 0, :], observations[0:1, :]], axis=0)
    lead = lax.all_gather(mine, "prow", axis=0)
    vmem = pl.BlockSpec(memory_space=pltpu.VMEM)
    smem = pl.BlockSpec(memory_space=pltpu.SMEM)
    slab, white, ll = pl.pallas_call(
        functools.partial(kernel, tile),
        out_shape=(
            jax.ShapeDtypeStruct((rows, SLAB_DEV), f32),
            jax.ShapeDtypeStruct((tile_count, tile), f32),
            jax.ShapeDtypeStruct((1, 1), f32),
        ),
        in_specs=[smem, smem, vmem, vmem, vmem],
        out_specs=(vmem, vmem, vmem),
        scratch_shapes=[
            pltpu.VMEM((n_lead, width), f32),
            pltpu.VMEM((n_lead, NB), f32),
            pltpu.VMEM((n_lead, NB), f32),
            pltpu.VMEM((rows, NB), f32),
            pltpu.VMEM((rows, n_lead), bf16),
            pltpu.VMEM((rows, n_lead), bf16),
            pltpu.VMEM((n_lead, 2 * NB), bf16),
            pltpu.VMEM((n_lead, 2 * NB), bf16),
            pltpu.VMEM((n_lead, 2 * NB), bf16),
            pltpu.VMEM((NB, NB), f32),
            pltpu.VMEM((NB, 2 * NB), bf16),
            pltpu.VMEM((NB, 2 * NB), bf16),
            pltpu.VMEM((n_lead - NB, 2 * NB), bf16),
            pltpu.VMEM((NB, width), bf16),
            pltpu.VMEM((NB, width), bf16),
        ],
        compiler_params=pltpu.CompilerParams(vmem_limit_bytes=48 * 1024 * 1024),
    )(length_scale, nugget, lead, coords.reshape(2, rows), observations)
    return slab.reshape(tile_count, tile, SLAB_DEV), white, ll.reshape(1)


def solution(mesh):
    placed = (P(None, None, "prow"), P(None, "prow"), P(), P())
    return jax.shard_map(
        shards,
        mesh=mesh,
        in_specs=placed,
        out_specs=(P(None, "prow", "pcol"), P(None, "prow"), P()),
        check_vma=False,
    )
```

```python
import functools

import jax
import jax.numpy as jnp
from jax import lax
from jax.experimental import pallas as pl
from jax.experimental.pallas import tpu as pltpu
from jax.sharding import PartitionSpec as P

SLAB_DEV = 128
NB = 128
SUB = 8


def lane_bcast(v, c):
    return jnp.broadcast_to(v[:, c : c + 1], v.shape)


def row_bcast(v, k):
    return jnp.broadcast_to(v[k : k + 1, :], v.shape)


def split2(x):
    hi = x.astype(jnp.bfloat16)
    lo = (x - hi.astype(jnp.float32)).astype(jnp.bfloat16)
    return hi, lo


def dot_f32(a, b):
    return jnp.dot(a, b, preferred_element_type=jnp.float32)


LOG2E = 1.4426950408889634


def matern(dx, dy, rate2):
    t = (dx * dx + dy * dy) * rate2
    s = t * lax.rsqrt(jnp.maximum(t, 1e-30))
    e = jnp.exp2(s * -LOG2E)
    return e + s * e


def tree_sum(xs):
    while len(xs) > 1:
        xs = [xs[i] + xs[i + 1] if i + 1 < len(xs) else xs[i] for i in range(0, len(xs), 2)]
    return xs[0]


def factor_block(rows, fill):
    sub = lax.broadcasted_iota(jnp.int32, (SUB, NB), 0)
    lane = lax.broadcasted_iota(jnp.int32, (SUB, NB), 1)
    units = [(sub == k).astype(jnp.float32) for k in range(SUB)]
    groups = len(rows)
    x_all = list(rows)
    out = []
    logs = jnp.zeros((SUB, NB), jnp.float32)
    cols = [lane_bcast(x_all[0], k) for k in range(SUB)]
    d = row_bcast(cols[0], 0)
    for s in range(groups):
        c0 = SUB * s
        more = s + 1 < groups
        if more:
            g_next = [lane_bcast(x_all[s + 1], c0 + k) for k in range(SUB)]
            low = list(g_next)
            ahead = [lane_bcast(x_all[s + 1], c0 + SUB + k) for k in range(SUB)]
        here = (lane >= c0) & (lane < c0 + SUB)
        x = jnp.where(here, (lane == sub + c0).astype(jnp.float32), x_all[s])
        x_out = jnp.zeros((SUB, NB), jnp.float32)
        prod = None
        for k in range(SUB):
            inv = pltpu.reciprocal(d, approx=True)
            rs = lax.rsqrt(d)
            prod = d if prod is None else prod * d
            if k + 1 < SUB:
                e = row_bcast(cols[k + 1], k)
                d = row_bcast(cols[k + 1], k + 1) - (e * e) * inv
            elif more:
                e = row_bcast(low[k], 0)
                d = row_bcast(ahead[0], 0) - (e * e) * inv
            f = cols[k] - units[k]
            fi = f * inv
            h = low[k] * inv if more else None
            for m in range(k + 1, SUB):
                e = row_bcast(cols[m], k)
                cols[m] = cols[m] - ((f * e) * inv if m <= k + 2 else fi * e)
                if more:
                    low[m] = low[m] - h * e
            if more:
                for m in range(SUB):
                    ahead[m] = ahead[m] - h * row_bcast(low[k], m)
            xk = row_bcast(x, k)
            x_out = jnp.where(sub == k, xk * rs, x_out)
            x = x - fi * xk
            fill(s, k)
        logs = logs + jnp.log(prod)
        out.append(jnp.where(lane < c0 + SUB, x_out, 0.0) if more else x_out)
        if more:
            x_rows = [row_bcast(x, k) for k in range(SUB)]
            for t in range(s + 1, groups):
                g = g_next if t == s + 1 else [
                    lane_bcast(x_all[t], c0 + k) for k in range(SUB)
                ]
                x_all[t] = jnp.where(here, 0.0, x_all[t]) - tree_sum(
                    [g[k] * x_rows[k] for k in range(SUB)]
                )
            cols = ahead
    return out, logs


def kernel(
    tile, ls_ref, ng_ref, lead_ref, loc_ref, obs_ref,
    slab_ref, white_ref, ll_ref,
    a_ref, z_ref, site_ref, row_ref, chi_ref, clo_ref, p1_ref, p2_ref, p3_ref,
    d_ref, winv_ref, pinv_ref, col_ref, mh_ref, ml_ref,
):
    f32, bf16 = jnp.float32, jnp.bfloat16
    n_lead = 2 * tile
    nblk = n_lead // NB
    width = n_lead + 2 * NB
    rows_total = loc_ref.shape[1]
    row_rank = lax.axis_index("prow")
    col_rank = lax.axis_index("pcol")
    row_procs = lax.axis_size("prow")
    ls = jnp.full((SUB, NB), ls_ref[0], f32)
    rate2 = 3.0 / (ls * ls)
    nugget = ng_ref[0]
    col_off = col_rank * SLAB_DEV
    col_tile = 2 + col_off // tile
    col_lane = pl.multiple_of(lax.rem(col_off, tile), SLAB_DEV)
    cx = lead_ref[col_tile, 0:1, pl.ds(col_lane, SLAB_DEV)]
    cy = lead_ref[col_tile, 1:2, pl.ds(col_lane, SLAB_DEV)]
    sub = lax.broadcasted_iota(jnp.int32, (SUB, NB), 0)
    lane = lax.broadcasted_iota(jnp.int32, (SUB, NB), 1)

    def columns(coord):
        pad = jnp.zeros((NB - coord.shape[0], NB), f32)
        return jnp.concatenate([coord, pad], axis=0).T

    def site_columns(q):
        t, o = divmod(q * NB, tile)
        site_ref[q * NB : (q + 1) * NB, :] = columns(lead_ref[t, :, o : o + NB])

    def row_columns(q):
        row_ref[q * NB : (q + 1) * NB, :] = columns(loc_ref[:, q * NB : (q + 1) * NB])

    held = {}

    def cov_piece(b, g, j):
        o = b * NB + g * SUB
        if ("site", o) not in held:
            v = site_ref[o : o + SUB, :]
            held["site", o] = [lane_bcast(v, c) for c in range(3)]
        x, y, ob = held["site", o]
        if j < nblk:
            t, u = divmod(j * NB, tile)
            val = matern(x - lead_ref[t, 0:1, u : u + NB], y - lead_ref[t, 1:2, u : u + NB], rate2)
            if j == b:
                val = jnp.where(lane == sub + g * SUB, val + nugget, val)
        elif j == nblk:
            val = matern(x - cx, y - cy, rate2)
        else:
            val = jnp.where(lane < 2, ob, 0.0)
        a_ref[o : o + SUB, j * NB : (j + 1) * NB] = val

    def row_piece(ro, key, j):
        if key not in held:
            held[key] = []
            for h in range(2):
                v = row_ref[pl.ds(pl.multiple_of(ro + h * SUB, SUB), SUB), :]
                held[key].append((lane_bcast(v, 0), lane_bcast(v, 1)))
        t, u = divmod(j * NB, tile)
        vals = [
            matern(x - lead_ref[t, 0:1, u : u + NB], y - lead_ref[t, 1:2, u : u + NB], rate2)
            for x, y in held[key]
        ]
        hi, lo = split2(jnp.concatenate(vals, axis=0))
        chi_ref[pl.ds(ro, 16), j * NB : (j + 1) * NB] = hi
        clo_ref[pl.ds(ro, 16), j * NB : (j + 1) * NB] = lo

    def three(al_parts, bh, bl):
        depth = bh.shape[0]
        return dot_f32(al_parts, jnp.concatenate([bh, bh], axis=0)) + dot_f32(
            al_parts[:, :depth], bl
        )

    def parts(x):
        return jnp.concatenate(split2(x), axis=1)

    def multiplier_piece(j0, j1):
        m = three(pinv_ref[...], *split2(a_ref[0:NB, j0:j1]))
        mh_ref[:, j0:j1], ml_ref[:, j0:j1] = split2(m)
        return m

    def column_parts():
        col_ref[...] = parts(a_ref[NB:n_lead, 0:NB])

    def update_piece(j0, j1, r0, r1, shift):
        new = a_ref[r0:r1, j0:j1] - three(
            col_ref[r0 - NB : r1 - NB, :], mh_ref[:, j0:j1], ml_ref[:, j0:j1]
        )
        a_ref[r0 - NB : r1 - NB, j0 - shift : j1 - shift] = new

    def tile_pieces(j0, j1, shift):
        box = {}

        def first():
            box["m"] = multiplier_piece(j0, j1)

        def last():
            a_ref[n_lead - NB : n_lead, j0 - shift : j1 - shift] = box["m"]

        half = (nblk // 2 + 1) * NB
        return [
            first,
            functools.partial(update_piece, j0, j1, NB, half, shift),
            functools.partial(update_piece, j0, j1, half, n_lead, shift),
            last,
        ]

    def keep_z(at):
        z_ref[pl.ds(at, NB), :] = three(
            winv_ref[...], *split2(a_ref[0:NB, n_lead + NB : width])
        )

    def finish_block(out, more_blocks):
        w = jnp.concatenate(out, axis=0)
        wt = w.T
        w_parts = parts(w)
        winv_ref[...] = w_parts
        wh, wl = w_parts[:, :NB], w_parts[:, NB:]
        if more_blocks:
            u = three(w_parts, *split2(a_ref[0:NB, NB : 2 * NB]))
            ut = three(parts(a_ref[NB : 2 * NB, 0:NB]), *split2(wt))
            d_ref[...] = a_ref[NB : 2 * NB, NB : 2 * NB] - three(parts(ut), *split2(u))
        pinv_ref[...] = parts(three(parts(wt), wh, wl))

    def load_rows():
        return [d_ref[SUB * t : SUB * (t + 1), :] for t in range(NB // SUB)]

    slots = (NB // SUB) * SUB

    def planned(urgent, work):
        plan = [[] for _ in range(slots)]
        early = slots * 7 // 8
        for i, f in enumerate(urgent):
            plan[i * early // len(urgent)].append(f)
        for i, f in enumerate(work):
            plan[i * slots // len(work)].append(f)

        def fill(s, k):
            for f in plan[s * SUB + k]:
                f()

        return fill

    for q in range(nblk):
        site_columns(q)
    for g in range(NB // SUB):
        cov_piece(0, g, 0)
    d_ref[...] = a_ref[0:NB, 0:NB]
    work = [
        functools.partial(cov_piece, b, g, j)
        for b in range(nblk)
        for g in range(NB // SUB)
        for j in range(nblk + 2)
        if (b, j) != (0, 0)
    ]
    urgent = [functools.partial(row_columns, q) for q in range(rows_total // NB)]
    out, logs = factor_block(load_rows(), planned(urgent, work))
    finish_block(out, True)

    chunk = -(-rows_total // 16 // (nblk - 1)) * 16
    col_tiles = [(j * NB, min(j + 2, nblk) * NB) for j in range(1, nblk, 2)]

    def step(b, logs):
        held.clear()
        base = jnp.minimum((b - 1) * chunk, rows_total - chunk)
        work = [
            functools.partial(
                row_piece, pl.multiple_of(base + pair * 16, 16), ("row", pair), j
            )
            for pair in range(chunk // 16)
            for j in range(nblk)
        ]
        urgent = [column_parts]
        for j0, j1 in col_tiles:
            urgent += tile_pieces(j0, j1, NB)
        urgent += [functools.partial(keep_z, pl.multiple_of((b - 1) * NB, NB))]
        urgent += tile_pieces(n_lead, width, 0)
        out, more = factor_block(load_rows(), planned(urgent, work))
        finish_block(out, True)
        return logs + more

    logs = lax.fori_loop(1, nblk, step, logs)
    column_parts()
    keep_z(n_lead - NB)
    for f in tile_pieces(n_lead, width, 0):
        f()

    y = a_ref[:, n_lead:width]
    yh, yl = split2(y)
    yt = ((y - yh.astype(f32)) - yl.astype(f32)).astype(bf16)
    first = lax.broadcasted_iota(jnp.int32, (n_lead, NB), 1) == 0
    p1_ref[...] = jnp.concatenate([yh[:, :NB], yl[:, :NB]], axis=1)
    obs_h, obs_l = yh[:, NB:].astype(f32), yl[:, NB:].astype(f32)
    p2_ref[...] = jnp.concatenate(
        [yt[:, :NB], jnp.where(first, obs_h, obs_l).astype(bf16)], axis=1
    )
    p3_ref[...] = jnp.concatenate(
        [yh[:, :NB], jnp.where(first, obs_h, 0.0).astype(bf16)], axis=1
    )

    z = z_ref[...]
    quad = 0.5 * jnp.sum(jnp.where(first, z * z, 0.0), keepdims=True)
    ll_ref[...] = -(quad + 0.5 * logs[0:1, 0:1]) / float(n_lead)

    big = 2 * NB
    for q in range(rows_total // big):
        o = q * big
        ch = chi_ref[o : o + big, :]
        acc = dot_f32(ch, p1_ref[...])
        acc2 = dot_f32(ch, p2_ref[...]) + dot_f32(clo_ref[o : o + big, :], p3_ref[...])
        corr = acc[:, :NB] + (acc[:, NB:] + acc2[:, :NB])
        t, off = divmod(o, tile)
        gid = (t * row_procs + row_rank) * tile + off
        leading = gid < n_lead
        v = row_ref[o : o + big, :]
        x = jnp.broadcast_to(v[:, 0:1], (big, NB))
        y = jnp.broadcast_to(v[:, 1:2], (big, NB))
        val = matern(x - cx, y - cy, rate2[0:1, :])
        rid = gid + lax.broadcasted_iota(jnp.int32, (big, NB), 0)
        cid = n_lead + col_off + lax.broadcasted_iota(jnp.int32, (big, NB), 1)
        val = jnp.where(rid == cid, val + nugget, val) - corr
        slab_ref[o : o + big, :] = jnp.where(leading, 0.0, val)
        for h in range(2):
            at = off + h * NB
            tr = acc2[h * NB : (h + 1) * NB, NB:].T
            rest = obs_ref[t : t + 1, at : at + NB] - (tr[0:1, :] + tr[1:2, :])
            if t == 0:
                zs = pl.multiple_of(jnp.where(leading, gid, 0) + h * NB, NB)
                zt = z_ref[pl.ds(zs, NB), :].T
                rest = jnp.where(leading, zt[0:1, :], rest)
            white_ref[t : t + 1, at : at + NB] = rest


def shards(coords, observations, length_scale, nugget):
    tile_count, tile = coords.shape[1:]
    rows = tile_count * tile
    n_lead = 2 * tile
    width = n_lead + 2 * NB
    f32, bf16 = jnp.float32, jnp.bfloat16
    mine = jnp.concatenate([coords[:, 0, :], observations[0:1, :]], axis=0)
    lead = lax.all_gather(mine, "prow", axis=0)
    vmem = pl.BlockSpec(memory_space=pltpu.VMEM)
    smem = pl.BlockSpec(memory_space=pltpu.SMEM)
    slab, white, ll = pl.pallas_call(
        functools.partial(kernel, tile),
        out_shape=(
            jax.ShapeDtypeStruct((rows, SLAB_DEV), f32),
            jax.ShapeDtypeStruct((tile_count, tile), f32),
            jax.ShapeDtypeStruct((1, 1), f32),
        ),
        in_specs=[smem, smem, vmem, vmem, vmem],
        out_specs=(vmem, vmem, vmem),
        scratch_shapes=[
            pltpu.VMEM((n_lead, width), f32),
            pltpu.VMEM((n_lead, NB), f32),
            pltpu.VMEM((n_lead, NB), f32),
            pltpu.VMEM((rows, NB), f32),
            pltpu.VMEM((rows, n_lead), bf16),
            pltpu.VMEM((rows, n_lead), bf16),
            pltpu.VMEM((n_lead, 2 * NB), bf16),
            pltpu.VMEM((n_lead, 2 * NB), bf16),
            pltpu.VMEM((n_lead, 2 * NB), bf16),
            pltpu.VMEM((NB, NB), f32),
            pltpu.VMEM((NB, 2 * NB), bf16),
            pltpu.VMEM((NB, 2 * NB), bf16),
            pltpu.VMEM((n_lead - NB, 2 * NB), bf16),
            pltpu.VMEM((NB, width), bf16),
            pltpu.VMEM((NB, width), bf16),
        ],
        compiler_params=pltpu.CompilerParams(vmem_limit_bytes=48 * 1024 * 1024),
    )(length_scale, nugget, lead, coords.reshape(2, rows), observations)
    return slab.reshape(tile_count, tile, SLAB_DEV), white, ll.reshape(1)


def solution(mesh):
    placed = (P(None, None, "prow"), P(None, "prow"), P(), P())
    return jax.shard_map(
        shards,
        mesh=mesh,
        in_specs=placed,
        out_specs=(P(None, "prow", "pcol"), P(None, "prow"), P()),
        check_vma=False,
    )
```

```python
import functools

import jax
import jax.numpy as jnp
from jax import lax
from jax.experimental import pallas as pl
from jax.experimental.pallas import tpu as pltpu
from jax.sharding import PartitionSpec as P

SLAB_DEV = 128
NB = 128
SUB = 8


def lane_bcast(v, c):
    return jnp.broadcast_to(v[:, c : c + 1], v.shape)


def row_bcast(v, k):
    return jnp.broadcast_to(v[k : k + 1, :], v.shape)


def split2(x):
    hi = x.astype(jnp.bfloat16)
    lo = (x - hi.astype(jnp.float32)).astype(jnp.bfloat16)
    return hi, lo


def dot_f32(a, b):
    return jnp.dot(a, b, preferred_element_type=jnp.float32)


LOG2E = 1.4426950408889634


def matern(dx, dy, rate2):
    t = (dx * dx + dy * dy) * rate2
    s = t * lax.rsqrt(jnp.maximum(t, 1e-30))
    e = jnp.exp2(s * -LOG2E)
    return e + s * e


def tree_sum(xs):
    while len(xs) > 1:
        xs = [xs[i] + xs[i + 1] if i + 1 < len(xs) else xs[i] for i in range(0, len(xs), 2)]
    return xs[0]


def factor_block(rows, fill):
    sub = lax.broadcasted_iota(jnp.int32, (SUB, NB), 0)
    lane = lax.broadcasted_iota(jnp.int32, (SUB, NB), 1)
    units = [(sub == k).astype(jnp.float32) for k in range(SUB)]
    groups = len(rows)
    x_all = list(rows)
    out = []
    logs = jnp.zeros((SUB, NB), jnp.float32)
    cols = [lane_bcast(x_all[0], k) for k in range(SUB)]
    d = row_bcast(cols[0], 0)
    for s in range(groups):
        c0 = SUB * s
        more = s + 1 < groups
        if more:
            g_next = [lane_bcast(x_all[s + 1], c0 + k) for k in range(SUB)]
            low = list(g_next)
            ahead = [lane_bcast(x_all[s + 1], c0 + SUB + k) for k in range(SUB)]
        here = (lane >= c0) & (lane < c0 + SUB)
        x = jnp.where(here, (lane == sub + c0).astype(jnp.float32), x_all[s])
        x_out = jnp.zeros((SUB, NB), jnp.float32)
        prod = None
        for k in range(SUB):
            inv = pltpu.reciprocal(d, approx=True)
            rs = lax.rsqrt(d)
            prod = d if prod is None else prod * d
            if k + 1 < SUB:
                e = row_bcast(cols[k + 1], k)
                d = row_bcast(cols[k + 1], k + 1) - (e * e) * inv
            elif more:
                e = row_bcast(low[k], 0)
                d = row_bcast(ahead[0], 0) - (e * e) * inv
            f = cols[k] - units[k]
            fi = f * inv
            h = low[k] * inv if more else None
            for m in range(k + 1, SUB):
                e = row_bcast(cols[m], k)
                cols[m] = cols[m] - ((f * e) * inv if m <= k + 2 else fi * e)
                if more:
                    low[m] = low[m] - h * e
            if more:
                for m in range(SUB):
                    ahead[m] = ahead[m] - h * row_bcast(low[k], m)
            xk = row_bcast(x, k)
            x_out = jnp.where(sub == k, xk * rs, x_out)
            x = x - fi * xk
            fill(s, k)
        logs = logs + jnp.log(prod)
        out.append(jnp.where(lane < c0 + SUB, x_out, 0.0) if more else x_out)
        if more:
            x_rows = [row_bcast(x, k) for k in range(SUB)]
            for t in range(s + 1, groups):
                g = g_next if t == s + 1 else [
                    lane_bcast(x_all[t], c0 + k) for k in range(SUB)
                ]
                x_all[t] = jnp.where(here, 0.0, x_all[t]) - tree_sum(
                    [g[k] * x_rows[k] for k in range(SUB)]
                )
            cols = ahead
    return out, logs


def kernel(
    peers, ls_ref, ng_ref, loc_ref, obs_ref, *refs,
):
    gathered, refs = refs[: max(2 * peers, 1)], refs[max(2 * peers, 1) :]
    (
        slab_ref, white_ref, ll_ref, lead_ref, a_ref, z_ref, site_ref, row_ref, chi_ref, clo_ref, p1_ref, p23_ref,
        d_ref, winv_ref, pinv_ref, col_ref, mh_ref, ml_ref,
    ) = refs
    f32, bf16 = jnp.float32, jnp.bfloat16
    tile_count, tile = obs_ref.shape
    n_lead = 2 * tile
    nblk = n_lead // NB
    width = n_lead + 2 * NB
    rows_total = tile_count * tile
    row_rank = lax.axis_index("prow")
    col_rank = lax.axis_index("pcol")
    row_procs = lax.axis_size("prow")
    if peers:
        for t in range(peers + 1):
            for c in range(3):
                own = loc_ref[c, 0:1, :] if c < 2 else obs_ref[0:1, :]
                for m in range(1, peers + 1):
                    xy_ref, ob_ref = gathered[m - 1], gathered[peers + m - 1]
                    theirs = xy_ref[c, 0:1, :] if c < 2 else ob_ref[0:1, :]
                    own = jnp.where(row_rank == t ^ m, theirs, own)
                lead_ref[t, c : c + 1, :] = own
    else:
        lead_ref[...] = gathered[0][...]
    ls = jnp.full((SUB, NB), ls_ref[0], f32)
    rate2 = 3.0 / (ls * ls)
    nugget = ng_ref[0]
    col_off = col_rank * SLAB_DEV
    col_tile = 2 + col_off // tile
    col_lane = pl.multiple_of(lax.rem(col_off, tile), SLAB_DEV)
    cx = lead_ref[col_tile, 0:1, pl.ds(col_lane, SLAB_DEV)]
    cy = lead_ref[col_tile, 1:2, pl.ds(col_lane, SLAB_DEV)]
    sub = lax.broadcasted_iota(jnp.int32, (SUB, NB), 0)
    lane = lax.broadcasted_iota(jnp.int32, (SUB, NB), 1)

    def columns(coord):
        pad = jnp.zeros((NB - coord.shape[0], NB), f32)
        return jnp.concatenate([coord, pad], axis=0).T

    def site_columns(q):
        t, o = divmod(q * NB, tile)
        site_ref[q * NB : (q + 1) * NB, :] = columns(lead_ref[t, :, o : o + NB])

    def row_columns(q):
        t, o = divmod(q * NB, tile)
        here = [loc_ref[c, t : t + 1, o : o + NB] for c in range(2)]
        row_ref[q * NB : (q + 1) * NB, :] = columns(jnp.concatenate(here, axis=0))

    held = {}

    def cov_piece(b, g, j):
        o = b * NB + g * SUB
        if ("site", o) not in held:
            v = site_ref[o : o + SUB, :]
            held["site", o] = [lane_bcast(v, c) for c in range(3)]
        x, y, ob = held["site", o]
        if j < nblk:
            t, u = divmod(j * NB, tile)
            val = matern(x - lead_ref[t, 0:1, u : u + NB], y - lead_ref[t, 1:2, u : u + NB], rate2)
            if j == b:
                val = jnp.where(lane == sub + g * SUB, val + nugget, val)
        elif j == nblk:
            val = matern(x - cx, y - cy, rate2)
        else:
            val = jnp.where(lane < 2, ob, 0.0)
        a_ref[o : o + SUB, j * NB : (j + 1) * NB] = val

    def row_piece(ro, key, j):
        if key not in held:
            held[key] = []
            for h in range(2):
                v = row_ref[pl.ds(pl.multiple_of(ro + h * SUB, SUB), SUB), :]
                held[key].append((lane_bcast(v, 0), lane_bcast(v, 1)))
        t, u = divmod(j * NB, tile)
        vals = [
            matern(x - lead_ref[t, 0:1, u : u + NB], y - lead_ref[t, 1:2, u : u + NB], rate2)
            for x, y in held[key]
        ]
        hi, lo = split2(jnp.concatenate(vals, axis=0))
        chi_ref[pl.ds(ro, 16), j * NB : (j + 1) * NB] = hi
        clo_ref[pl.ds(ro, 16), j * NB : (j + 1) * NB] = lo

    def three(al_parts, bh, bl):
        return dot_f32(al_parts, jnp.concatenate([bh, bh, bl], axis=0))

    def parts(x):
        h, l = split2(x)
        return jnp.concatenate([h, l, h], axis=1)

    def multiplier_piece(j0, j1):
        m = three(pinv_ref[...], *split2(a_ref[0:NB, j0:j1]))
        mh_ref[:, j0:j1], ml_ref[:, j0:j1] = split2(m)
        return m

    def column_parts():
        col_ref[...] = parts(a_ref[NB:n_lead, 0:NB])

    def update_piece(j0, j1, r0, r1, shift):
        new = a_ref[r0:r1, j0:j1] - three(
            col_ref[r0 - NB : r1 - NB, :], mh_ref[:, j0:j1], ml_ref[:, j0:j1]
        )
        a_ref[r0 - NB : r1 - NB, j0 - shift : j1 - shift] = new

    def tile_pieces(j0, j1, shift):
        box = {}

        def first():
            box["m"] = multiplier_piece(j0, j1)

        def last():
            a_ref[n_lead - NB : n_lead, j0 - shift : j1 - shift] = box["m"]

        half = (nblk // 2 + 1) * NB
        return [
            first,
            functools.partial(update_piece, j0, j1, NB, half, shift),
            functools.partial(update_piece, j0, j1, half, n_lead, shift),
            last,
        ]

    def keep_z(at):
        z_ref[pl.ds(at, NB), :] = three(
            winv_ref[...], *split2(a_ref[0:NB, n_lead + NB : width])
        )

    def finish_block(out, more_blocks):
        w = jnp.concatenate(out, axis=0)
        wt = w.T
        w_parts = parts(w)
        winv_ref[...] = w_parts
        wh, wl = w_parts[:, :NB], w_parts[:, NB : 2 * NB]
        if more_blocks:
            u = three(w_parts, *split2(a_ref[0:NB, NB : 2 * NB]))
            ut = three(parts(a_ref[NB : 2 * NB, 0:NB]), *split2(wt))
            d_ref[...] = a_ref[NB : 2 * NB, NB : 2 * NB] - three(parts(ut), *split2(u))
        pinv_ref[...] = parts(three(parts(wt), wh, wl))

    def load_rows():
        return [d_ref[SUB * t : SUB * (t + 1), :] for t in range(NB // SUB)]

    slots = (NB // SUB) * SUB

    def planned(urgent, work):
        plan = [[] for _ in range(slots)]
        early = slots * 7 // 8
        for i, f in enumerate(urgent):
            plan[i * early // len(urgent)].append(f)
        for i, f in enumerate(work):
            plan[i * slots // len(work)].append(f)

        def fill(s, k):
            for f in plan[s * SUB + k]:
                f()

        return fill

    for q in range(nblk):
        site_columns(q)
    for g in range(NB // SUB):
        cov_piece(0, g, 0)
    d_ref[...] = a_ref[0:NB, 0:NB]
    work = [
        functools.partial(cov_piece, b, g, j)
        for b in range(nblk)
        for g in range(NB // SUB)
        for j in range(nblk + 2)
        if (b, j) != (0, 0)
    ]
    urgent = [functools.partial(row_columns, q) for q in range(rows_total // NB)]
    out, logs = factor_block(load_rows(), planned(urgent, work))
    finish_block(out, True)

    chunk = -(-rows_total // 16 // (nblk - 1)) * 16
    col_tiles = [(j * NB, min(j + 2, nblk) * NB) for j in range(1, nblk, 2)]

    def step(b, logs):
        held.clear()
        base = jnp.minimum((b - 1) * chunk, rows_total - chunk)
        work = [
            functools.partial(
                row_piece, pl.multiple_of(base + pair * 16, 16), ("row", pair), j
            )
            for pair in range(chunk // 16)
            for j in range(nblk)
        ]
        urgent = [column_parts]
        for j0, j1 in col_tiles:
            urgent += tile_pieces(j0, j1, NB)
        urgent += [functools.partial(keep_z, pl.multiple_of((b - 1) * NB, NB))]
        urgent += tile_pieces(n_lead, width, 0)
        out, more = factor_block(load_rows(), planned(urgent, work))
        finish_block(out, True)
        return logs + more

    logs = lax.fori_loop(1, nblk, step, logs)
    column_parts()
    keep_z(n_lead - NB)
    for f in tile_pieces(n_lead, width, 0):
        f()

    y = a_ref[:, n_lead:width]
    yh, yl = split2(y)
    yt = ((y - yh.astype(f32)) - yl.astype(f32)).astype(bf16)
    first = lax.broadcasted_iota(jnp.int32, (n_lead, NB), 1) == 0
    p1_ref[...] = jnp.concatenate([yh[:, :NB], yl[:, :NB]], axis=1)
    obs_h, obs_l = yh[:, NB:].astype(f32), yl[:, NB:].astype(f32)
    p23_ref[0:n_lead, :] = jnp.concatenate(
        [yt[:, :NB], jnp.where(first, obs_h, obs_l).astype(bf16)], axis=1
    )
    p23_ref[n_lead : 2 * n_lead, :] = jnp.concatenate(
        [yh[:, :NB], jnp.where(first, obs_h, 0.0).astype(bf16)], axis=1
    )

    z = z_ref[...]
    quad = 0.5 * jnp.sum(jnp.where(first, z * z, 0.0), keepdims=True)
    ll_ref[...] = -(quad + 0.5 * logs[0:1, 0:1]) / float(n_lead)

    big = tile
    for q in range(rows_total // big):
        o = q * big
        ch = chi_ref[o : o + big, :]
        acc = dot_f32(ch, p1_ref[...])
        acc2 = dot_f32(jnp.concatenate([ch, clo_ref[o : o + big, :]], axis=1), p23_ref[...])
        corr = acc[:, :NB] + (acc[:, NB:] + acc2[:, :NB])
        t, off = divmod(o, tile)
        gid = (t * row_procs + row_rank) * tile + off
        leading = gid < n_lead
        v = row_ref[o : o + big, :]
        x = jnp.broadcast_to(v[:, 0:1], (big, NB))
        y = jnp.broadcast_to(v[:, 1:2], (big, NB))
        val = matern(x - cx, y - cy, rate2[0:1, :])
        rid = gid + lax.broadcasted_iota(jnp.int32, (big, NB), 0)
        cid = n_lead + col_off + lax.broadcasted_iota(jnp.int32, (big, NB), 1)
        val = jnp.where(rid == cid, val + nugget, val) - corr
        slab_ref[o : o + big, :] = jnp.where(leading, 0.0, val)
        for h in range(big // NB):
            at = off + h * NB
            tr = acc2[h * NB : (h + 1) * NB, NB:].T
            rest = obs_ref[t : t + 1, at : at + NB] - (tr[0:1, :] + tr[1:2, :])
            if t == 0:
                zs = pl.multiple_of(jnp.where(leading, gid, 0) + h * NB, NB)
                zt = z_ref[pl.ds(zs, NB), :].T
                rest = jnp.where(leading, zt[0:1, :], rest)
            white_ref[t : t + 1, at : at + NB] = rest


def shards(coords, observations, length_scale, nugget):
    tile_count, tile = coords.shape[1:]
    rows = tile_count * tile
    n_lead = 2 * tile
    width = n_lead + 2 * NB
    f32, bf16 = jnp.float32, jnp.bfloat16
    procs = lax.axis_size("prow")
    if procs <= 4 and procs & (procs - 1) == 0:
        peers = procs - 1
        gathered = [
            lax.ppermute(x, "prow", [(r, r ^ m) for r in range(procs)])
            for x in (coords, observations)
            for m in range(1, procs)
        ]
    else:
        peers = 0
        mine = jnp.concatenate([coords[:, 0, :], observations[0:1, :]], axis=0)
        gathered = [lax.all_gather(mine, "prow", axis=0)]
    vmem = pl.BlockSpec(memory_space=pltpu.VMEM)
    smem = pl.BlockSpec(memory_space=pltpu.SMEM)
    slab, white, ll = pl.pallas_call(
        functools.partial(kernel, peers),
        out_shape=(
            jax.ShapeDtypeStruct((rows, SLAB_DEV), f32),
            jax.ShapeDtypeStruct((tile_count, tile), f32),
            jax.ShapeDtypeStruct((1, 1), f32),
        ),
        in_specs=[smem, smem] + [vmem] * (2 + len(gathered)),
        out_specs=(vmem, vmem, vmem),
        scratch_shapes=[
            pltpu.VMEM((procs, 3, tile), f32),
            pltpu.VMEM((n_lead, width), f32),
            pltpu.VMEM((n_lead, NB), f32),
            pltpu.VMEM((n_lead, NB), f32),
            pltpu.VMEM((rows, NB), f32),
            pltpu.VMEM((rows, n_lead), bf16),
            pltpu.VMEM((rows, n_lead), bf16),
            pltpu.VMEM((n_lead, 2 * NB), bf16),
            pltpu.VMEM((2 * n_lead, 2 * NB), bf16),
            pltpu.VMEM((NB, NB), f32),
            pltpu.VMEM((NB, 3 * NB), bf16),
            pltpu.VMEM((NB, 3 * NB), bf16),
            pltpu.VMEM((n_lead - NB, 3 * NB), bf16),
            pltpu.VMEM((NB, width), bf16),
            pltpu.VMEM((NB, width), bf16),
        ],
        compiler_params=pltpu.CompilerParams(vmem_limit_bytes=48 * 1024 * 1024),
    )(length_scale, nugget, coords, observations, *gathered)
    return slab.reshape(tile_count, tile, SLAB_DEV), white, ll.reshape(1)


def solution(mesh):
    placed = (P(None, None, "prow"), P(None, "prow"), P(), P())
    return jax.shard_map(
        shards,
        mesh=mesh,
        in_specs=placed,
        out_specs=(P(None, "prow", "pcol"), P(None, "prow"), P()),
        check_vma=False,
    )
```

```python
import functools

import jax
import jax.numpy as jnp
from jax import lax
from jax.experimental import pallas as pl
from jax.experimental.pallas import tpu as pltpu
from jax.sharding import PartitionSpec as P

SLAB_DEV = 128
NB = 128
SUB = 8


def lane_bcast(v, c):
    return jnp.broadcast_to(v[:, c : c + 1], v.shape)


def row_bcast(v, k):
    return jnp.broadcast_to(v[k : k + 1, :], v.shape)


def split2(x):
    hi = x.astype(jnp.bfloat16)
    lo = (x - hi.astype(jnp.float32)).astype(jnp.bfloat16)
    return hi, lo


def dot_f32(a, b):
    return jnp.dot(a, b, preferred_element_type=jnp.float32)


LOG2E = 1.4426950408889634


def matern(dx, dy, rate2):
    t = (dx * dx + dy * dy) * rate2
    s = t * lax.rsqrt(jnp.maximum(t, 1e-30))
    e = jnp.exp2(s * -LOG2E)
    return e + s * e


def tree_sum(xs):
    while len(xs) > 1:
        xs = [xs[i] + xs[i + 1] if i + 1 < len(xs) else xs[i] for i in range(0, len(xs), 2)]
    return xs[0]


def factor_block(rows, fill):
    sub = lax.broadcasted_iota(jnp.int32, (SUB, NB), 0)
    lane = lax.broadcasted_iota(jnp.int32, (SUB, NB), 1)
    units = [(sub == k).astype(jnp.float32) for k in range(SUB)]
    groups = len(rows)
    x_all = list(rows)
    out = []
    logs = jnp.zeros((SUB, NB), jnp.float32)
    cols = [lane_bcast(x_all[0], k) for k in range(SUB)]
    d = row_bcast(cols[0], 0)
    for s in range(groups):
        c0 = SUB * s
        more = s + 1 < groups
        if more:
            g_next = [lane_bcast(x_all[s + 1], c0 + k) for k in range(SUB)]
            low = list(g_next)
            ahead = [lane_bcast(x_all[s + 1], c0 + SUB + k) for k in range(SUB)]
        here = (lane >= c0) & (lane < c0 + SUB)
        x = jnp.where(here, (lane == sub + c0).astype(jnp.float32), x_all[s])
        x_out = jnp.zeros((SUB, NB), jnp.float32)
        prod = None
        for k in range(SUB):
            inv = pltpu.reciprocal(d, approx=True)
            rs = lax.rsqrt(d)
            prod = d if prod is None else prod * d
            if k + 1 < SUB:
                e = row_bcast(cols[k + 1], k)
                d = row_bcast(cols[k + 1], k + 1) - (e * e) * inv
            elif more:
                e = row_bcast(low[k], 0)
                d = row_bcast(ahead[0], 0) - (e * e) * inv
            f = cols[k] - units[k]
            fi = f * inv
            h = low[k] * inv if more else None
            for m in range(k + 1, SUB):
                e = row_bcast(cols[m], k)
                cols[m] = cols[m] - ((f * e) * inv if m <= k + 2 else fi * e)
                if more:
                    low[m] = low[m] - h * e
            if more:
                for m in range(SUB):
                    ahead[m] = ahead[m] - h * row_bcast(low[k], m)
            xk = row_bcast(x, k)
            x_out = jnp.where(sub == k, xk * rs, x_out)
            x = x - fi * xk
            fill(s, k)
        logs = logs + jnp.log(prod)
        out.append(jnp.where(lane < c0 + SUB, x_out, 0.0) if more else x_out)
        if more:
            x_rows = [row_bcast(x, k) for k in range(SUB)]
            for t in range(s + 1, groups):
                g = g_next if t == s + 1 else [
                    lane_bcast(x_all[t], c0 + k) for k in range(SUB)
                ]
                x_all[t] = jnp.where(here, 0.0, x_all[t]) - tree_sum(
                    [g[k] * x_rows[k] for k in range(SUB)]
                )
            cols = ahead
    return out, logs


def kernel(
    peers, ls_ref, ng_ref, loc_ref, *refs,
):
    gathered, refs = refs[: peers + 1], refs[peers + 1 :]
    (
        slab_ref, white_ref, ll_ref, lead_ref, a_ref, z_ref, site_ref, row_ref, chi_ref, clo_ref, p1_ref, p23_ref,
        d_ref, winv_ref, pinv_ref, col_ref, mh_ref, ml_ref,
    ) = refs
    f32, bf16 = jnp.float32, jnp.bfloat16
    tile_count, tile = loc_ref.shape[1:]
    n_lead = 2 * tile
    nblk = n_lead // NB
    width = n_lead + 2 * NB
    rows_total = tile_count * tile
    row_rank = lax.axis_index("prow")
    col_rank = lax.axis_index("pcol")
    row_procs = lax.axis_size("prow")
    if peers:
        for t in range(peers + 1):
            rows = gathered[0][...]
            for m in range(1, peers + 1):
                rows = jnp.where(row_rank == t ^ m, gathered[m][...], rows)
            lead_ref[t] = rows
    else:
        lead_ref[...] = gathered[0][...]
    ls = jnp.full((SUB, NB), ls_ref[0], f32)
    rate2 = 3.0 / (ls * ls)
    nugget = ng_ref[0]
    col_off = col_rank * SLAB_DEV
    col_tile = 2 + col_off // tile
    col_lane = pl.multiple_of(lax.rem(col_off, tile), SLAB_DEV)
    cx = lead_ref[col_tile, 0:1, pl.ds(col_lane, SLAB_DEV)]
    cy = lead_ref[col_tile, 1:2, pl.ds(col_lane, SLAB_DEV)]
    sub = lax.broadcasted_iota(jnp.int32, (SUB, NB), 0)
    lane = lax.broadcasted_iota(jnp.int32, (SUB, NB), 1)

    def columns(coord):
        pad = jnp.zeros((NB - coord.shape[0], NB), f32)
        return jnp.concatenate([coord, pad], axis=0).T

    def site_columns(q):
        t, o = divmod(q * NB, tile)
        site_ref[q * NB : (q + 1) * NB, :] = columns(lead_ref[t, :, o : o + NB])

    def row_columns(q):
        t, o = divmod(q * NB, tile)
        here = [loc_ref[c, t : t + 1, o : o + NB] for c in range(2)]
        row_ref[q * NB : (q + 1) * NB, :] = columns(jnp.concatenate(here, axis=0))

    held = {}

    def cov_piece(b, g, j):
        o = b * NB + g * SUB
        if ("site", o) not in held:
            v = site_ref[o : o + SUB, :]
            held["site", o] = [lane_bcast(v, c) for c in range(3)]
        x, y, ob = held["site", o]
        if j < nblk:
            t, u = divmod(j * NB, tile)
            val = matern(x - lead_ref[t, 0:1, u : u + NB], y - lead_ref[t, 1:2, u : u + NB], rate2)
            if j == b:
                val = jnp.where(lane == sub + g * SUB, val + nugget, val)
        elif j == nblk:
            val = matern(x - cx, y - cy, rate2)
        else:
            val = jnp.where(lane < 2, ob, 0.0)
        a_ref[o : o + SUB, j * NB : (j + 1) * NB] = val

    def row_piece(ro, key, j):
        if key not in held:
            held[key] = []
            for h in range(2):
                at = ro + h * SUB
                v = row_ref[pl.ds(at if isinstance(at, int) else pl.multiple_of(at, SUB), SUB), :]
                held[key].append((lane_bcast(v, 0), lane_bcast(v, 1)))
        t, u = divmod(j * NB, tile)
        vals = [
            matern(x - lead_ref[t, 0:1, u : u + NB], y - lead_ref[t, 1:2, u : u + NB], rate2)
            for x, y in held[key]
        ]
        hi, lo = split2(jnp.concatenate(vals, axis=0))
        chi_ref[pl.ds(ro, 16), j * NB : (j + 1) * NB] = hi
        clo_ref[pl.ds(ro, 16), j * NB : (j + 1) * NB] = lo

    def three(al_parts, bh, bl):
        return dot_f32(al_parts, jnp.concatenate([bh, bh, bl], axis=0))

    def parts(x):
        h, l = split2(x)
        return jnp.concatenate([h, l, h], axis=1)

    def multiplier_piece(j0, j1):
        m = three(pinv_ref[...], *split2(a_ref[0:NB, j0:j1]))
        mh_ref[:, j0:j1], ml_ref[:, j0:j1] = split2(m)
        return m

    def column_parts():
        col_ref[...] = parts(a_ref[NB:n_lead, 0:NB])

    def update_piece(j0, j1, r0, r1, shift):
        new = a_ref[r0:r1, j0:j1] - three(
            col_ref[r0 - NB : r1 - NB, :], mh_ref[:, j0:j1], ml_ref[:, j0:j1]
        )
        a_ref[r0 - NB : r1 - NB, j0 - shift : j1 - shift] = new

    def tile_pieces(j0, j1, shift):
        box = {}

        def first():
            box["m"] = multiplier_piece(j0, j1)

        def last():
            a_ref[n_lead - NB : n_lead, j0 - shift : j1 - shift] = box["m"]

        half = (nblk // 2 + 1) * NB
        return [
            first,
            functools.partial(update_piece, j0, j1, NB, half, shift),
            functools.partial(update_piece, j0, j1, half, n_lead, shift),
            last,
        ]

    def keep_z(at):
        z_ref[pl.ds(at, NB), :] = three(
            winv_ref[...], *split2(a_ref[0:NB, n_lead + NB : width])
        )

    def finish_block(out, more_blocks):
        w = jnp.concatenate(out, axis=0)
        wt = w.T
        w_parts = parts(w)
        winv_ref[...] = w_parts
        wh, wl = w_parts[:, :NB], w_parts[:, NB : 2 * NB]
        if more_blocks:
            u = three(w_parts, *split2(a_ref[0:NB, NB : 2 * NB]))
            ut = three(parts(a_ref[NB : 2 * NB, 0:NB]), *split2(wt))
            d_ref[...] = a_ref[NB : 2 * NB, NB : 2 * NB] - three(parts(ut), *split2(u))
        pinv_ref[...] = parts(three(parts(wt), wh, wl))

    def load_rows():
        return [d_ref[SUB * t : SUB * (t + 1), :] for t in range(NB // SUB)]

    slots = (NB // SUB) * SUB

    def planned(urgent, work):
        plan = [[] for _ in range(slots)]
        early = slots * 7 // 8
        for i, f in enumerate(urgent):
            plan[i * early // len(urgent)].append(f)
        for i, f in enumerate(work):
            plan[i * slots // len(work)].append(f)

        def fill(s, k):
            for f in plan[s * SUB + k]:
                f()

        return fill

    for q in range(nblk):
        site_columns(q)
    for g in range(NB // SUB):
        cov_piece(0, g, 0)
    d_ref[...] = a_ref[0:NB, 0:NB]
    work = [
        functools.partial(cov_piece, b, g, j)
        for b in range(nblk)
        for g in range(NB // SUB)
        for j in range(nblk + 2)
        if (b, j) != (0, 0)
    ]
    urgent = [functools.partial(row_columns, q) for q in range(rows_total // NB)]
    out, logs = factor_block(load_rows(), planned(urgent, work))
    finish_block(out, True)

    big = 2 * NB
    early_rows = rows_total * 3 // 4 // big * big
    chunk = -(-early_rows // 16 // (nblk - 1)) * 16
    col_tiles = [(j * NB, min(j + 2, nblk) * NB) for j in range(1, nblk, 2)]

    def step(b, logs):
        held.clear()
        base = jnp.minimum((b - 1) * chunk, early_rows - chunk)
        work = [
            functools.partial(
                row_piece, pl.multiple_of(base + pair * 16, 16), ("row", pair), j
            )
            for pair in range(chunk // 16)
            for j in range(nblk)
        ]
        urgent = [column_parts]
        for j0, j1 in col_tiles:
            urgent += tile_pieces(j0, j1, NB)
        urgent += [functools.partial(keep_z, pl.multiple_of((b - 1) * NB, NB))]
        urgent += tile_pieces(n_lead, width, 0)
        out, more = factor_block(load_rows(), planned(urgent, work))
        finish_block(out, True)
        return logs + more

    logs = lax.fori_loop(1, nblk, step, logs)
    column_parts()
    keep_z(n_lead - NB)
    for f in tile_pieces(n_lead, width, 0):
        f()

    y = a_ref[:, n_lead:width]
    yh, yl = split2(y)
    yt = ((y - yh.astype(f32)) - yl.astype(f32)).astype(bf16)
    first = lax.broadcasted_iota(jnp.int32, (n_lead, NB), 1) == 0
    p1_ref[...] = jnp.concatenate([yh[:, :NB], yl[:, :NB]], axis=1)
    obs_h, obs_l = yh[:, NB:].astype(f32), yl[:, NB:].astype(f32)
    p23_ref[0:n_lead, :] = jnp.concatenate(
        [yt[:, :NB], jnp.where(first, obs_h, obs_l).astype(bf16)], axis=1
    )
    p23_ref[n_lead : 2 * n_lead, :] = jnp.concatenate(
        [yh[:, :NB], jnp.where(first, obs_h, 0.0).astype(bf16)], axis=1
    )

    z = z_ref[...]
    quad = 0.5 * jnp.sum(jnp.where(first, z * z, 0.0), keepdims=True)
    ll_ref[...] = -(quad + 0.5 * logs[0:1, 0:1]) / float(n_lead)

    held.clear()
    late = [
        functools.partial(row_piece, ro, ("late", ro), j)
        for ro in range(early_rows, rows_total, 16)
        for j in range(nblk)
    ]
    turns = early_rows // big
    for q in range(rows_total // big):
        o = q * big
        for f in late[len(late) * q // turns : len(late) * (q + 1) // turns]:
            f()
        ch = chi_ref[o : o + big, :]
        acc = dot_f32(ch, p1_ref[...])
        acc2 = dot_f32(jnp.concatenate([ch, clo_ref[o : o + big, :]], axis=1), p23_ref[...])
        corr = acc[:, :NB] + (acc[:, NB:] + acc2[:, :NB])
        t, off = divmod(o, tile)
        gid = (t * row_procs + row_rank) * tile + off
        leading = gid < n_lead
        v = row_ref[o : o + big, :]
        x = jnp.broadcast_to(v[:, 0:1], (big, NB))
        y = jnp.broadcast_to(v[:, 1:2], (big, NB))
        val = matern(x - cx, y - cy, rate2[0:1, :])
        rid = gid + lax.broadcasted_iota(jnp.int32, (big, NB), 0)
        cid = n_lead + col_off + lax.broadcasted_iota(jnp.int32, (big, NB), 1)
        val = jnp.where(rid == cid, val + nugget, val) - corr
        slab_ref[o : o + big, :] = jnp.where(leading, 0.0, val)
        for h in range(big // NB):
            at = off + h * NB
            tr = acc2[h * NB : (h + 1) * NB, NB:].T
            rest = loc_ref[2, t : t + 1, at : at + NB] - (tr[0:1, :] + tr[1:2, :])
            if t == 0:
                zs = pl.multiple_of(jnp.where(leading, gid, 0) + h * NB, NB)
                zt = z_ref[pl.ds(zs, NB), :].T
                rest = jnp.where(leading, zt[0:1, :], rest)
            white_ref[t : t + 1, at : at + NB] = rest


def shards(coords, observations, length_scale, nugget):
    tile_count, tile = coords.shape[1:]
    rows = tile_count * tile
    n_lead = 2 * tile
    width = n_lead + 2 * NB
    f32, bf16 = jnp.float32, jnp.bfloat16
    procs = lax.axis_size("prow")
    local = lax.optimization_barrier(jnp.concatenate([coords, observations[None]], axis=0))
    mine = local[:, 0, :]
    if procs <= 4 and procs & (procs - 1) == 0:
        peers = procs - 1
        gathered = [mine] + [
            lax.ppermute(mine, "prow", [(r, r ^ m) for r in range(procs)])
            for m in range(1, procs)
        ]
    else:
        peers = 0
        gathered = [lax.all_gather(mine, "prow", axis=0)]
    vmem = pl.BlockSpec(memory_space=pltpu.VMEM)
    smem = pl.BlockSpec(memory_space=pltpu.SMEM)
    slab, white, ll = pl.pallas_call(
        functools.partial(kernel, peers),
        out_shape=(
            jax.ShapeDtypeStruct((rows, SLAB_DEV), f32),
            jax.ShapeDtypeStruct((tile_count, tile), f32),
            jax.ShapeDtypeStruct((1, 1), f32),
        ),
        in_specs=[smem, smem, vmem] + [vmem] * len(gathered),
        out_specs=(vmem, vmem, vmem),
        scratch_shapes=[
            pltpu.VMEM((procs, 3, tile), f32),
            pltpu.VMEM((n_lead, width), f32),
            pltpu.VMEM((n_lead, NB), f32),
            pltpu.VMEM((n_lead, NB), f32),
            pltpu.VMEM((rows, NB), f32),
            pltpu.VMEM((rows, n_lead), bf16),
            pltpu.VMEM((rows, n_lead), bf16),
            pltpu.VMEM((n_lead, 2 * NB), bf16),
            pltpu.VMEM((2 * n_lead, 2 * NB), bf16),
            pltpu.VMEM((NB, NB), f32),
            pltpu.VMEM((NB, 3 * NB), bf16),
            pltpu.VMEM((NB, 3 * NB), bf16),
            pltpu.VMEM((n_lead - NB, 3 * NB), bf16),
            pltpu.VMEM((NB, width), bf16),
            pltpu.VMEM((NB, width), bf16),
        ],
        compiler_params=pltpu.CompilerParams(vmem_limit_bytes=48 * 1024 * 1024),
    )(length_scale, nugget, local, *gathered)
    return slab.reshape(tile_count, tile, SLAB_DEV), white, ll.reshape(1)


def solution(mesh):
    placed = (P(None, None, "prow"), P(None, "prow"), P(), P())
    return jax.shard_map(
        shards,
        mesh=mesh,
        in_specs=placed,
        out_specs=(P(None, "prow", "pcol"), P(None, "prow"), P()),
        check_vma=False,
    )
```

```python
import functools

import jax
import jax.numpy as jnp
from jax import lax
from jax.experimental import pallas as pl
from jax.experimental.pallas import tpu as pltpu
from jax.sharding import PartitionSpec as P

SLAB_DEV = 128
NB = 128
SUB = 8


def lane_bcast(v, c):
    return jnp.broadcast_to(v[:, c : c + 1], v.shape)


def row_bcast(v, k):
    return jnp.broadcast_to(v[k : k + 1, :], v.shape)


def split2(x):
    hi = x.astype(jnp.bfloat16)
    lo = (x - hi.astype(jnp.float32)).astype(jnp.bfloat16)
    return hi, lo


def dot_f32(a, b):
    return jnp.dot(a, b, preferred_element_type=jnp.float32)


LOG2E = 1.4426950408889634


def matern(dx, dy, rate2):
    t = (dx * dx + dy * dy) * rate2
    s = t * lax.rsqrt(jnp.maximum(t, 1e-30))
    e = jnp.exp2(s * -LOG2E)
    return e + s * e


def tree_sum(xs):
    while len(xs) > 1:
        xs = [xs[i] + xs[i + 1] if i + 1 < len(xs) else xs[i] for i in range(0, len(xs), 2)]
    return xs[0]


def factor_block(rows, fill):
    sub = lax.broadcasted_iota(jnp.int32, (SUB, NB), 0)
    lane = lax.broadcasted_iota(jnp.int32, (SUB, NB), 1)
    units = [(sub == k).astype(jnp.float32) for k in range(SUB)]
    groups = len(rows)
    x_all = list(rows)
    out = []
    logs = jnp.zeros((SUB, NB), jnp.float32)
    cols = [lane_bcast(x_all[0], k) for k in range(SUB)]
    pivot = row_bcast(cols[0], 0), row_bcast(cols[1], 0), row_bcast(cols[1], 1)
    for s in range(groups):
        c0 = SUB * s
        more = s + 1 < groups
        if more:
            g_next = [lane_bcast(x_all[s + 1], c0 + k) for k in range(SUB)]
            low = list(g_next)
            ahead = [lane_bcast(x_all[s + 1], c0 + SUB + k) for k in range(SUB)]
        here = (lane >= c0) & (lane < c0 + SUB)
        x = jnp.where(here, (lane == sub + c0).astype(jnp.float32), x_all[s])
        x_out = jnp.zeros((SUB, NB), jnp.float32)
        prod = None
        for k in range(0, SUB, 2):
            a, b, c = pivot
            det = a * c - b * b
            inv = pltpu.reciprocal(det, approx=True)
            prod = det if prod is None else prod * det
            pairs = [(row_bcast(cols[m], k), row_bcast(cols[m], k + 1)) for m in range(k + 2, SUB)]
            nxt = None
            if k + 2 < SUB:
                m0, m1 = cols[k + 2], cols[k + 3]
                nxt = pairs[0], pairs[1], k + 2
            elif more:
                m0, m1 = ahead[0], ahead[1]
                nxt = [(row_bcast(low[k], m), row_bcast(low[k + 1], m)) for m in range(2)] + [0]
            if nxt is not None:
                (p0, q0), (p1, q1), at = nxt
                u0, v0 = c * p0 - b * q0, a * q0 - b * p0
                u1, v1 = c * p1 - b * q1, a * q1 - b * p1
                pivot = (
                    row_bcast(m0, at) - (u0 * p0 + v0 * q0) * inv,
                    row_bcast(m1, at) - (u0 * p1 + v0 * q1) * inv,
                    row_bcast(m1, at + 1) - (u1 * p1 + v1 * q1) * inv,
                )
            f0, f1 = cols[k] - units[k], cols[k + 1] - units[k + 1]
            g0, g1 = f0 * c - f1 * b, f1 * a - f0 * b
            e0, e1 = g0 * inv, g1 * inv
            if more:
                l0, l1 = low[k], low[k + 1]
                h0, h1 = (l0 * c - l1 * b) * inv, (l1 * a - l0 * b) * inv
            for m in range(k + 2, SUB):
                p, q = pairs[m - k - 2]
                cols[m] = cols[m] - (
                    (g0 * p + g1 * q) * inv if m < k + 4 else e0 * p + e1 * q
                )
                if more:
                    low[m] = low[m] - (h0 * p + h1 * q)
            if more:
                for m in range(SUB):
                    ahead[m] = ahead[m] - (h0 * row_bcast(l0, m) + h1 * row_bcast(l1, m))
            x0, x1 = row_bcast(x, k), row_bcast(x, k + 1)
            rs0 = lax.rsqrt(a)
            inv_a = rs0 * rs0
            rs1 = lax.rsqrt(det * inv_a)
            x_out = jnp.where(sub == k, x0 * rs0, x_out)
            x_out = jnp.where(sub == k + 1, (x1 - (b * inv_a) * x0) * rs1, x_out)
            x = x - (e0 * x0 + e1 * x1)
            fill(s, k)
            fill(s, k + 1)
        logs = logs + jnp.log(prod)
        out.append(jnp.where(lane < c0 + SUB, x_out, 0.0) if more else x_out)
        if more:
            x_rows = [row_bcast(x, k) for k in range(SUB)]
            for t in range(s + 1, groups):
                g = g_next if t == s + 1 else [
                    lane_bcast(x_all[t], c0 + k) for k in range(SUB)
                ]
                x_all[t] = jnp.where(here, 0.0, x_all[t]) - tree_sum(
                    [g[k] * x_rows[k] for k in range(SUB)]
                )
            cols = ahead
    return out, logs


def kernel(
    peers, ls_ref, ng_ref, loc_ref, *refs,
):
    gathered, refs = refs[: peers + 1], refs[peers + 1 :]
    (
        slab_ref, white_ref, ll_ref, lead_ref, a_ref, z_ref, site_ref, row_ref, chi_ref, clo_ref, p1_ref, p23_ref,
        d_ref, winv_ref, pinv_ref, col_ref, mh_ref, ml_ref,
    ) = refs
    f32, bf16 = jnp.float32, jnp.bfloat16
    tile_count, tile = loc_ref.shape[1:]
    n_lead = 2 * tile
    nblk = n_lead // NB
    width = n_lead + 2 * NB
    rows_total = tile_count * tile
    row_rank = lax.axis_index("prow")
    col_rank = lax.axis_index("pcol")
    row_procs = lax.axis_size("prow")
    if peers:
        for t in range(peers + 1):
            rows = gathered[0][...]
            for m in range(1, peers + 1):
                rows = jnp.where(row_rank == t ^ m, gathered[m][...], rows)
            lead_ref[t] = rows
    else:
        lead_ref[...] = gathered[0][...]
    ls = jnp.full((SUB, NB), ls_ref[0], f32)
    rate2 = 3.0 / (ls * ls)
    nugget = ng_ref[0]
    col_off = col_rank * SLAB_DEV
    col_tile = 2 + col_off // tile
    col_lane = pl.multiple_of(lax.rem(col_off, tile), SLAB_DEV)
    cx = lead_ref[col_tile, 0:1, pl.ds(col_lane, SLAB_DEV)]
    cy = lead_ref[col_tile, 1:2, pl.ds(col_lane, SLAB_DEV)]
    sub = lax.broadcasted_iota(jnp.int32, (SUB, NB), 0)
    lane = lax.broadcasted_iota(jnp.int32, (SUB, NB), 1)

    def columns(coord):
        pad = jnp.zeros((NB - coord.shape[0], NB), f32)
        return jnp.concatenate([coord, pad], axis=0).T

    def site_columns(q):
        t, o = divmod(q * NB, tile)
        site_ref[q * NB : (q + 1) * NB, :] = columns(lead_ref[t, :, o : o + NB])

    def row_columns(q):
        t, o = divmod(q * NB, tile)
        here = [loc_ref[c, t : t + 1, o : o + NB] for c in range(2)]
        row_ref[q * NB : (q + 1) * NB, :] = columns(jnp.concatenate(here, axis=0))

    held = {}

    def cov_piece(b, g, j):
        o = b * NB + g * SUB
        if ("site", o) not in held:
            v = site_ref[o : o + SUB, :]
            held["site", o] = [lane_bcast(v, c) for c in range(3)]
        x, y, ob = held["site", o]
        if j < nblk:
            t, u = divmod(j * NB, tile)
            val = matern(x - lead_ref[t, 0:1, u : u + NB], y - lead_ref[t, 1:2, u : u + NB], rate2)
            if j == b:
                val = jnp.where(lane == sub + g * SUB, val + nugget, val)
        elif j == nblk:
            val = matern(x - cx, y - cy, rate2)
        else:
            val = jnp.where(lane < 2, ob, 0.0)
        a_ref[o : o + SUB, j * NB : (j + 1) * NB] = val

    def row_piece(ro, key, j):
        if key not in held:
            held[key] = []
            for h in range(2):
                at = ro + h * SUB
                v = row_ref[pl.ds(at if isinstance(at, int) else pl.multiple_of(at, SUB), SUB), :]
                held[key].append((lane_bcast(v, 0), lane_bcast(v, 1)))
        t, u = divmod(j * NB, tile)
        vals = [
            matern(x - lead_ref[t, 0:1, u : u + NB], y - lead_ref[t, 1:2, u : u + NB], rate2)
            for x, y in held[key]
        ]
        hi, lo = split2(jnp.concatenate(vals, axis=0))
        chi_ref[pl.ds(ro, 16), j * NB : (j + 1) * NB] = hi
        clo_ref[pl.ds(ro, 16), j * NB : (j + 1) * NB] = lo

    def three(al_parts, bh, bl):
        return dot_f32(al_parts, jnp.concatenate([bh, bh, bl], axis=0))

    def parts(x):
        h, l = split2(x)
        return jnp.concatenate([h, l, h], axis=1)

    def multiplier_piece(j0, j1):
        m = three(pinv_ref[...], *split2(a_ref[0:NB, j0:j1]))
        mh_ref[:, j0:j1], ml_ref[:, j0:j1] = split2(m)
        return m

    def column_parts():
        col_ref[...] = parts(a_ref[NB:n_lead, 0:NB])

    def update_piece(j0, j1, r0, r1, shift):
        new = a_ref[r0:r1, j0:j1] - three(
            col_ref[r0 - NB : r1 - NB, :], mh_ref[:, j0:j1], ml_ref[:, j0:j1]
        )
        a_ref[r0 - NB : r1 - NB, j0 - shift : j1 - shift] = new

    def tile_pieces(j0, j1, shift):
        box = {}

        def first():
            box["m"] = multiplier_piece(j0, j1)

        def last():
            a_ref[n_lead - NB : n_lead, j0 - shift : j1 - shift] = box["m"]

        half = (nblk // 2 + 1) * NB
        return [
            first,
            functools.partial(update_piece, j0, j1, NB, half, shift),
            functools.partial(update_piece, j0, j1, half, n_lead, shift),
            last,
        ]

    def keep_z(at):
        z_ref[pl.ds(at, NB), :] = three(
            winv_ref[...], *split2(a_ref[0:NB, n_lead + NB : width])
        )

    def finish_block(out, more_blocks):
        w = jnp.concatenate(out, axis=0)
        wt = w.T
        w_parts = parts(w)
        winv_ref[...] = w_parts
        wh, wl = w_parts[:, :NB], w_parts[:, NB : 2 * NB]
        if more_blocks:
            u = three(w_parts, *split2(a_ref[0:NB, NB : 2 * NB]))
            ut = three(parts(a_ref[NB : 2 * NB, 0:NB]), *split2(wt))
            d_ref[...] = a_ref[NB : 2 * NB, NB : 2 * NB] - three(parts(ut), *split2(u))
        pinv_ref[...] = parts(three(parts(wt), wh, wl))

    def load_rows():
        return [d_ref[SUB * t : SUB * (t + 1), :] for t in range(NB // SUB)]

    slots = (NB // SUB) * SUB

    def planned(urgent, work):
        plan = [[] for _ in range(slots)]
        early = slots * 7 // 8
        for i, f in enumerate(urgent):
            plan[i * early // len(urgent)].append(f)
        for i, f in enumerate(work):
            plan[i * slots // len(work)].append(f)

        def fill(s, k):
            for f in plan[s * SUB + k]:
                f()

        return fill

    for q in range(nblk):
        site_columns(q)
    for g in range(NB // SUB):
        cov_piece(0, g, 0)
    d_ref[...] = a_ref[0:NB, 0:NB]
    work = [
        functools.partial(cov_piece, b, g, j)
        for b in range(nblk)
        for g in range(NB // SUB)
        for j in range(nblk + 2)
        if (b, j) != (0, 0)
    ]
    urgent = [functools.partial(row_columns, q) for q in range(rows_total // NB)]
    out, logs = factor_block(load_rows(), planned(urgent, work))
    finish_block(out, True)

    big = 2 * NB
    early_rows = rows_total * 3 // 4 // big * big
    chunk = -(-early_rows // 16 // (nblk - 1)) * 16
    col_tiles = [(j * NB, min(j + 2, nblk) * NB) for j in range(1, nblk, 2)]

    def step(b, logs):
        held.clear()
        base = jnp.minimum((b - 1) * chunk, early_rows - chunk)
        work = [
            functools.partial(
                row_piece, pl.multiple_of(base + pair * 16, 16), ("row", pair), j
            )
            for pair in range(chunk // 16)
            for j in range(nblk)
        ]
        urgent = [column_parts]
        for j0, j1 in col_tiles:
            urgent += tile_pieces(j0, j1, NB)
        urgent += [functools.partial(keep_z, pl.multiple_of((b - 1) * NB, NB))]
        urgent += tile_pieces(n_lead, width, 0)
        out, more = factor_block(load_rows(), planned(urgent, work))
        finish_block(out, True)
        return logs + more

    logs = lax.fori_loop(1, nblk, step, logs)
    column_parts()
    keep_z(n_lead - NB)
    for f in tile_pieces(n_lead, width, 0):
        f()

    y = a_ref[:, n_lead:width]
    yh, yl = split2(y)
    yt = ((y - yh.astype(f32)) - yl.astype(f32)).astype(bf16)
    first = lax.broadcasted_iota(jnp.int32, (n_lead, NB), 1) == 0
    p1_ref[...] = jnp.concatenate([yh[:, :NB], yl[:, :NB]], axis=1)
    obs_h, obs_l = yh[:, NB:].astype(f32), yl[:, NB:].astype(f32)
    p23_ref[0:n_lead, :] = jnp.concatenate(
        [yt[:, :NB], jnp.where(first, obs_h, obs_l).astype(bf16)], axis=1
    )
    p23_ref[n_lead : 2 * n_lead, :] = jnp.concatenate(
        [yh[:, :NB], jnp.where(first, obs_h, 0.0).astype(bf16)], axis=1
    )

    z = z_ref[...]
    quad = 0.5 * jnp.sum(jnp.where(first, z * z, 0.0), keepdims=True)
    ll_ref[...] = -(quad + 0.5 * logs[0:1, 0:1]) / float(n_lead)

    held.clear()
    late = [
        functools.partial(row_piece, ro, ("late", ro), j)
        for ro in range(early_rows, rows_total, 16)
        for j in range(nblk)
    ]
    turns = early_rows // big
    for q in range(rows_total // big):
        o = q * big
        for f in late[len(late) * q // turns : len(late) * (q + 1) // turns]:
            f()
        ch = chi_ref[o : o + big, :]
        acc = dot_f32(ch, p1_ref[...])
        acc2 = dot_f32(jnp.concatenate([ch, clo_ref[o : o + big, :]], axis=1), p23_ref[...])
        corr = acc[:, :NB] + (acc[:, NB:] + acc2[:, :NB])
        t, off = divmod(o, tile)
        gid = (t * row_procs + row_rank) * tile + off
        leading = gid < n_lead
        v = row_ref[o : o + big, :]
        x = jnp.broadcast_to(v[:, 0:1], (big, NB))
        y = jnp.broadcast_to(v[:, 1:2], (big, NB))
        val = matern(x - cx, y - cy, rate2[0:1, :])
        rid = gid + lax.broadcasted_iota(jnp.int32, (big, NB), 0)
        cid = n_lead + col_off + lax.broadcasted_iota(jnp.int32, (big, NB), 1)
        val = jnp.where(rid == cid, val + nugget, val) - corr
        slab_ref[o : o + big, :] = jnp.where(leading, 0.0, val)
        for h in range(big // NB):
            at = off + h * NB
            tr = acc2[h * NB : (h + 1) * NB, NB:].T
            rest = loc_ref[2, t : t + 1, at : at + NB] - (tr[0:1, :] + tr[1:2, :])
            if t == 0:
                zs = pl.multiple_of(jnp.where(leading, gid, 0) + h * NB, NB)
                zt = z_ref[pl.ds(zs, NB), :].T
                rest = jnp.where(leading, zt[0:1, :], rest)
            white_ref[t : t + 1, at : at + NB] = rest


def shards(coords, observations, length_scale, nugget):
    tile_count, tile = coords.shape[1:]
    rows = tile_count * tile
    n_lead = 2 * tile
    width = n_lead + 2 * NB
    f32, bf16 = jnp.float32, jnp.bfloat16
    procs = lax.axis_size("prow")
    local = lax.optimization_barrier(jnp.concatenate([coords, observations[None]], axis=0))
    mine = local[:, 0, :]
    if procs <= 4 and procs & (procs - 1) == 0:
        peers = procs - 1
        gathered = [mine] + [
            lax.ppermute(mine, "prow", [(r, r ^ m) for r in range(procs)])
            for m in range(1, procs)
        ]
    else:
        peers = 0
        gathered = [lax.all_gather(mine, "prow", axis=0)]
    vmem = pl.BlockSpec(memory_space=pltpu.VMEM)
    smem = pl.BlockSpec(memory_space=pltpu.SMEM)
    slab, white, ll = pl.pallas_call(
        functools.partial(kernel, peers),
        out_shape=(
            jax.ShapeDtypeStruct((rows, SLAB_DEV), f32),
            jax.ShapeDtypeStruct((tile_count, tile), f32),
            jax.ShapeDtypeStruct((1, 1), f32),
        ),
        in_specs=[smem, smem, vmem] + [vmem] * len(gathered),
        out_specs=(vmem, vmem, vmem),
        scratch_shapes=[
            pltpu.VMEM((procs, 3, tile), f32),
            pltpu.VMEM((n_lead, width), f32),
            pltpu.VMEM((n_lead, NB), f32),
            pltpu.VMEM((n_lead, NB), f32),
            pltpu.VMEM((rows, NB), f32),
            pltpu.VMEM((rows, n_lead), bf16),
            pltpu.VMEM((rows, n_lead), bf16),
            pltpu.VMEM((n_lead, 2 * NB), bf16),
            pltpu.VMEM((2 * n_lead, 2 * NB), bf16),
            pltpu.VMEM((NB, NB), f32),
            pltpu.VMEM((NB, 3 * NB), bf16),
            pltpu.VMEM((NB, 3 * NB), bf16),
            pltpu.VMEM((n_lead - NB, 3 * NB), bf16),
            pltpu.VMEM((NB, width), bf16),
            pltpu.VMEM((NB, width), bf16),
        ],
        compiler_params=pltpu.CompilerParams(vmem_limit_bytes=48 * 1024 * 1024),
    )(length_scale, nugget, local, *gathered)
    return slab.reshape(tile_count, tile, SLAB_DEV), white, ll.reshape(1)


def solution(mesh):
    placed = (P(None, None, "prow"), P(None, "prow"), P(), P())
    return jax.shard_map(
        shards,
        mesh=mesh,
        in_specs=placed,
        out_specs=(P(None, "prow", "pcol"), P(None, "prow"), P()),
        check_vma=False,
    )
```

```python
import functools
import math

import jax
import jax.numpy as jnp
from jax import lax
from jax.experimental import pallas as pl
from jax.experimental.pallas import tpu as pltpu
from jax.sharding import PartitionSpec as P

SLAB_DEV = 128
NB = 128
SUB = 8
AHEAD = 4


def lane_bcast(v, c):
    return jnp.broadcast_to(v[:, c : c + 1], v.shape)


def row_bcast(v, k):
    return jnp.broadcast_to(v[k : k + 1, :], v.shape)


def split2(x):
    hi = x.astype(jnp.bfloat16)
    lo = (x - hi.astype(jnp.float32)).astype(jnp.bfloat16)
    return hi, lo


def dot_f32(a, b):
    return jnp.dot(a, b, preferred_element_type=jnp.float32)


LOG2E = 1.4426950408889634


def matern(dx, dy, rate):
    d2 = dx * dx + dy * dy
    dist = d2 * lax.rsqrt(jnp.maximum(d2, 1e-30))
    e = jnp.exp2(dist * rate[1])
    return e + (dist * rate[0]) * e


def tree_sum(xs):
    while len(xs) > 1:
        xs = [xs[i] + xs[i + 1] if i + 1 < len(xs) else xs[i] for i in range(0, len(xs), 2)]
    return xs[0]


def factor_block(rows, fill):
    sub = lax.broadcasted_iota(jnp.int32, (SUB, NB), 0)
    lane = lax.broadcasted_iota(jnp.int32, (SUB, NB), 1)
    units = [(sub == k).astype(jnp.float32) for k in range(SUB)]
    groups = len(rows)
    x_all = list(rows)
    out = []
    logs = jnp.zeros((SUB, NB), jnp.float32)
    cols = [lane_bcast(x_all[0], k) for k in range(SUB)]
    d = row_bcast(cols[0], 0)
    for s in range(groups):
        c0 = SUB * s
        more = s + 1 < groups
        if more:
            low = [lane_bcast(x_all[s + 1], c0 + k) for k in range(SUB)]
            ahead = [lane_bcast(x_all[s + 1], c0 + SUB + k) for k in range(AHEAD)]
        here = (lane >= c0) & (lane < c0 + SUB)
        x = jnp.where(here, (lane == sub + c0).astype(jnp.float32), x_all[s])
        if more:
            x_next = jnp.where(here, 0.0, x_all[s + 1])
        x_out = jnp.zeros((SUB, NB), jnp.float32)
        prod = None
        for k in range(SUB):
            inv = pltpu.reciprocal(d, approx=True)
            rs = lax.rsqrt(d)
            prod = d if prod is None else prod * d
            if k + 1 < SUB:
                e = row_bcast(cols[k + 1], k)
                d = row_bcast(cols[k + 1], k + 1) - (e * e) * inv
            elif more:
                e = row_bcast(low[k], 0)
                d = row_bcast(ahead[0], 0) - (e * e) * inv
            f = cols[k] - units[k]
            fi = f * inv
            h = low[k] * inv if more else None
            for m in range(k + 1, SUB):
                e = row_bcast(cols[m], k)
                cols[m] = cols[m] - ((f * e) * inv if m <= k + 2 else fi * e)
                if more:
                    low[m] = low[m] - h * e
            if more:
                for m in range(AHEAD):
                    ahead[m] = ahead[m] - h * row_bcast(low[k], m)
            xk = row_bcast(x, k)
            if more:
                x_next = x_next - h * xk
            x_out = jnp.where(sub == k, xk * rs, x_out)
            x = x - fi * xk
            fill(s, k)
        logs = logs + jnp.log(prod)
        out.append(jnp.where(lane < c0 + SUB, x_out, 0.0) if more else x_out)
        if more:
            x_rows = [row_bcast(x, k) for k in range(SUB)]
            for t in range(s + 2, groups):
                g = [lane_bcast(x_all[t], c0 + k) for k in range(SUB)]
                x_all[t] = jnp.where(here, 0.0, x_all[t]) - tree_sum(
                    [g[k] * x_rows[k] for k in range(SUB)]
                )
            x_all[s + 1] = x_next
            cols = ahead + [lane_bcast(x_next, c0 + SUB + k) for k in range(AHEAD, SUB)]
    return out, logs


def kernel(
    peers, ls_ref, ng_ref, loc_ref, *refs,
):
    gathered, refs = refs[: peers + 1], refs[peers + 1 :]
    (
        slab_hbm, white_ref, ll_ref, slab_ref, sems, lead_ref, a_ref, z_ref, site_ref, row_ref, chi_ref, clo_ref, p1_ref, p23_ref,
        d_ref, winv_ref, pinv_ref, col_ref, mh_ref, ml_ref,
    ) = refs
    f32, bf16 = jnp.float32, jnp.bfloat16
    tile_count, tile = loc_ref.shape[1:]
    n_lead = 2 * tile
    nblk = n_lead // NB
    width = n_lead + 2 * NB
    rows_total = tile_count * tile
    row_rank = lax.axis_index("prow")
    col_rank = lax.axis_index("pcol")
    row_procs = lax.axis_size("prow")
    if peers:
        for t in range(peers + 1):
            rows = gathered[0][...]
            for m in range(1, peers + 1):
                rows = jnp.where(row_rank == t ^ m, gathered[m][...], rows)
            lead_ref[t] = rows
    else:
        lead_ref[...] = gathered[0][...]
    ls = jnp.full((SUB, NB), ls_ref[0], f32)
    decay = math.sqrt(3.0) / ls
    rate = decay, decay * -LOG2E
    nugget = ng_ref[0]
    col_off = col_rank * SLAB_DEV
    col_tile = 2 + col_off // tile
    col_lane = pl.multiple_of(lax.rem(col_off, tile), SLAB_DEV)
    cx = lead_ref[col_tile, 0:1, pl.ds(col_lane, SLAB_DEV)]
    cy = lead_ref[col_tile, 1:2, pl.ds(col_lane, SLAB_DEV)]
    sub = lax.broadcasted_iota(jnp.int32, (SUB, NB), 0)
    lane = lax.broadcasted_iota(jnp.int32, (SUB, NB), 1)

    def columns(coord):
        pad = jnp.zeros((NB - coord.shape[0], NB), f32)
        return jnp.concatenate([coord, pad], axis=0).T

    def site_columns(q):
        t, o = divmod(q * NB, tile)
        site_ref[q * NB : (q + 1) * NB, :] = columns(lead_ref[t, :, o : o + NB])

    def row_columns(q):
        t, o = divmod(q * NB, tile)
        here = [loc_ref[c, t : t + 1, o : o + NB] for c in range(2)]
        row_ref[q * NB : (q + 1) * NB, :] = columns(jnp.concatenate(here, axis=0))

    held = {}

    def cov_piece(b, g, j):
        o = b * NB + g * SUB
        if ("site", o) not in held:
            v = site_ref[o : o + SUB, :]
            held["site", o] = [lane_bcast(v, c) for c in range(3)]
        x, y, ob = held["site", o]
        if j < nblk:
            t, u = divmod(j * NB, tile)
            val = matern(x - lead_ref[t, 0:1, u : u + NB], y - lead_ref[t, 1:2, u : u + NB], rate)
            if j == b:
                val = jnp.where(lane == sub + g * SUB, val + nugget, val)
        elif j == nblk:
            val = matern(x - cx, y - cy, rate)
        else:
            val = jnp.where(lane < 2, ob, 0.0)
        a_ref[o : o + SUB, j * NB : (j + 1) * NB] = val

    def row_piece(ro, key, j):
        if key not in held:
            held[key] = []
            for h in range(2):
                at = ro + h * SUB
                v = row_ref[pl.ds(at if isinstance(at, int) else pl.multiple_of(at, SUB), SUB), :]
                held[key].append((lane_bcast(v, 0), lane_bcast(v, 1)))
        t, u = divmod(j * NB, tile)
        vals = [
            matern(x - lead_ref[t, 0:1, u : u + NB], y - lead_ref[t, 1:2, u : u + NB], rate)
            for x, y in held[key]
        ]
        hi, lo = split2(jnp.concatenate(vals, axis=0))
        chi_ref[pl.ds(ro, 16), j * NB : (j + 1) * NB] = hi
        clo_ref[pl.ds(ro, 16), j * NB : (j + 1) * NB] = lo

    def three(al_parts, bh, bl):
        return dot_f32(al_parts, jnp.concatenate([bh, bh, bl], axis=0))

    def parts(x):
        h, l = split2(x)
        return jnp.concatenate([h, l, h], axis=1)

    def multiplier_piece(j0, j1):
        m = three(pinv_ref[...], *split2(a_ref[0:NB, j0:j1]))
        mh_ref[:, j0:j1], ml_ref[:, j0:j1] = split2(m)
        return m

    def column_parts():
        col_ref[...] = parts(a_ref[NB:n_lead, 0:NB])

    def update_piece(j0, j1, r0, r1, shift):
        new = a_ref[r0:r1, j0:j1] - three(
            col_ref[r0 - NB : r1 - NB, :], mh_ref[:, j0:j1], ml_ref[:, j0:j1]
        )
        a_ref[r0 - NB : r1 - NB, j0 - shift : j1 - shift] = new

    def tile_pieces(j0, j1, shift):
        box = {}

        def first():
            box["m"] = multiplier_piece(j0, j1)

        def last():
            a_ref[n_lead - NB : n_lead, j0 - shift : j1 - shift] = box["m"]

        half = (nblk // 2 + 1) * NB
        return [
            first,
            functools.partial(update_piece, j0, j1, NB, half, shift),
            functools.partial(update_piece, j0, j1, half, n_lead, shift),
            last,
        ]

    def keep_z(at):
        z_ref[pl.ds(at, NB), :] = three(
            winv_ref[...], *split2(a_ref[0:NB, n_lead + NB : width])
        )

    def finish_block(out, more_blocks):
        w = jnp.concatenate(out, axis=0)
        wt = w.T
        w_parts = parts(w)
        winv_ref[...] = w_parts
        wh, wl = w_parts[:, :NB], w_parts[:, NB : 2 * NB]
        if more_blocks:
            u = three(w_parts, *split2(a_ref[0:NB, NB : 2 * NB]))
            ut = three(parts(a_ref[NB : 2 * NB, 0:NB]), *split2(wt))
            d_ref[...] = a_ref[NB : 2 * NB, NB : 2 * NB] - three(parts(ut), *split2(u))
        pinv_ref[...] = parts(three(parts(wt), wh, wl))

    def load_rows():
        return [d_ref[SUB * t : SUB * (t + 1), :] for t in range(NB // SUB)]

    slots = (NB // SUB) * SUB

    def planned(urgent, work):
        plan = [[] for _ in range(slots)]
        early = slots * 7 // 8
        for i, f in enumerate(urgent):
            plan[i * early // len(urgent)].append(f)
        for i, f in enumerate(work):
            plan[i * slots // len(work)].append(f)

        def fill(s, k):
            for f in plan[s * SUB + k]:
                f()

        return fill

    for q in range(nblk):
        site_columns(q)
    for g in range(NB // SUB):
        cov_piece(0, g, 0)
    d_ref[...] = a_ref[0:NB, 0:NB]
    work = [
        functools.partial(cov_piece, b, g, j)
        for b in range(nblk)
        for g in range(NB // SUB)
        for j in range(nblk + 2)
        if (b, j) != (0, 0)
    ]
    urgent = [functools.partial(row_columns, q) for q in range(rows_total // NB)]
    out, logs = factor_block(load_rows(), planned(urgent, work))
    finish_block(out, True)

    big = 2 * NB
    early_rows = rows_total * 3 // 4 // big * big
    chunk = -(-early_rows // 16 // (nblk - 1)) * 16

    def step(upto, b, logs):
        col_tiles = [(j * NB, min(j + 2, upto) * NB) for j in range(1, upto, 2)]
        held.clear()
        base = jnp.minimum((b - 1) * chunk, early_rows - chunk)
        work = [
            functools.partial(
                row_piece, pl.multiple_of(base + pair * 16, 16), ("row", pair), j
            )
            for pair in range(chunk // 16)
            for j in range(nblk)
        ]
        urgent = [column_parts]
        for j0, j1 in col_tiles:
            urgent += tile_pieces(j0, j1, NB)
        urgent += [functools.partial(keep_z, pl.multiple_of((b - 1) * NB, NB))]
        urgent += tile_pieces(n_lead, width, 0)
        out, more = factor_block(load_rows(), planned(urgent, work))
        finish_block(out, True)
        return logs + more

    mid = nblk // 2
    logs = lax.fori_loop(1, mid, functools.partial(step, nblk), logs)
    logs = lax.fori_loop(mid, nblk, functools.partial(step, nblk - mid + 1), logs)
    column_parts()
    keep_z(n_lead - NB)
    for f in tile_pieces(n_lead, width, 0):
        f()

    y = a_ref[:, n_lead:width]
    yh, yl = split2(y)
    yt = ((y - yh.astype(f32)) - yl.astype(f32)).astype(bf16)
    first = lax.broadcasted_iota(jnp.int32, (n_lead, NB), 1) == 0
    p1_ref[...] = jnp.concatenate([yh[:, :NB], yl[:, :NB]], axis=1)
    obs_h, obs_l = yh[:, NB:].astype(f32), yl[:, NB:].astype(f32)
    p23_ref[0:n_lead, :] = jnp.concatenate(
        [yt[:, :NB], jnp.where(first, obs_h, obs_l).astype(bf16)], axis=1
    )
    p23_ref[n_lead : 2 * n_lead, :] = jnp.concatenate(
        [yh[:, :NB], jnp.where(first, obs_h, 0.0).astype(bf16)], axis=1
    )

    z = z_ref[...]
    quad = 0.5 * jnp.sum(jnp.where(first, z * z, 0.0), keepdims=True)
    ll_ref[...] = -(quad + 0.5 * logs[0:1, 0:1]) / float(n_lead)

    held.clear()
    late = [
        functools.partial(row_piece, ro, ("late", ro), j)
        for ro in range(early_rows, rows_total, 16)
        for j in range(nblk)
    ]
    turns = early_rows // big
    copies = []
    for q in range(rows_total // big):
        o = q * big
        for f in late[len(late) * q // turns : len(late) * (q + 1) // turns]:
            f()
        ch = chi_ref[o : o + big, :]
        acc = dot_f32(ch, p1_ref[...])
        acc2 = dot_f32(jnp.concatenate([ch, clo_ref[o : o + big, :]], axis=1), p23_ref[...])
        corr = acc[:, :NB] + (acc[:, NB:] + acc2[:, :NB])
        t, off = divmod(o, tile)
        gid = (t * row_procs + row_rank) * tile + off
        leading = gid < n_lead
        v = row_ref[o : o + big, :]
        x = jnp.broadcast_to(v[:, 0:1], (big, NB))
        y = jnp.broadcast_to(v[:, 1:2], (big, NB))
        val = matern(x - cx, y - cy, (rate[0][0:1, :], rate[1][0:1, :]))
        rid = gid + lax.broadcasted_iota(jnp.int32, (big, NB), 0)
        cid = n_lead + col_off + lax.broadcasted_iota(jnp.int32, (big, NB), 1)
        val = jnp.where(rid == cid, val + nugget, val) - corr
        slab_ref[o : o + big, :] = jnp.where(leading, 0.0, val)
        copies.append(
            pltpu.make_async_copy(
                slab_ref.at[pl.ds(o, big)], slab_hbm.at[pl.ds(o, big)], sems.at[q]
            )
        )
        copies[-1].start()
        for h in range(big // NB):
            at = off + h * NB
            tr = acc2[h * NB : (h + 1) * NB, NB:].T
            rest = loc_ref[2, t : t + 1, at : at + NB] - (tr[0:1, :] + tr[1:2, :])
            if t == 0:
                zs = pl.multiple_of(jnp.where(leading, gid, 0) + h * NB, NB)
                zt = z_ref[pl.ds(zs, NB), :].T
                rest = jnp.where(leading, zt[0:1, :], rest)
            white_ref[t : t + 1, at : at + NB] = rest
    for copy in copies:
        copy.wait()


def shards(coords, observations, length_scale, nugget):
    tile_count, tile = coords.shape[1:]
    rows = tile_count * tile
    n_lead = 2 * tile
    width = n_lead + 2 * NB
    f32, bf16 = jnp.float32, jnp.bfloat16
    procs = lax.axis_size("prow")
    local = lax.optimization_barrier(jnp.concatenate([coords, observations[None]], axis=0))
    mine = local[:, 0, :]
    if procs <= 4 and procs & (procs - 1) == 0:
        peers = procs - 1
        gathered = [mine] + [
            lax.ppermute(mine, "prow", [(r, r ^ m) for r in range(procs)])
            for m in range(1, procs)
        ]
    else:
        peers = 0
        gathered = [lax.all_gather(mine, "prow", axis=0)]
    vmem = pl.BlockSpec(memory_space=pltpu.VMEM)
    smem = pl.BlockSpec(memory_space=pltpu.SMEM)
    slab, white, ll = pl.pallas_call(
        functools.partial(kernel, peers),
        out_shape=(
            jax.ShapeDtypeStruct((rows, SLAB_DEV), f32),
            jax.ShapeDtypeStruct((tile_count, tile), f32),
            jax.ShapeDtypeStruct((1, 1), f32),
        ),
        in_specs=[smem, smem, vmem] + [vmem] * len(gathered),
        out_specs=(pl.BlockSpec(memory_space=pl.ANY), vmem, vmem),
        scratch_shapes=[
            pltpu.VMEM((rows, SLAB_DEV), f32),
            pltpu.SemaphoreType.DMA((rows // (2 * NB),)),
            pltpu.VMEM((procs, 3, tile), f32),
            pltpu.VMEM((n_lead, width), f32),
            pltpu.VMEM((n_lead, NB), f32),
            pltpu.VMEM((n_lead, NB), f32),
            pltpu.VMEM((rows, NB), f32),
            pltpu.VMEM((rows, n_lead), bf16),
            pltpu.VMEM((rows, n_lead), bf16),
            pltpu.VMEM((n_lead, 2 * NB), bf16),
            pltpu.VMEM((2 * n_lead, 2 * NB), bf16),
            pltpu.VMEM((NB, NB), f32),
            pltpu.VMEM((NB, 3 * NB), bf16),
            pltpu.VMEM((NB, 3 * NB), bf16),
            pltpu.VMEM((n_lead - NB, 3 * NB), bf16),
            pltpu.VMEM((NB, width), bf16),
            pltpu.VMEM((NB, width), bf16),
        ],
        compiler_params=pltpu.CompilerParams(vmem_limit_bytes=48 * 1024 * 1024),
    )(length_scale, nugget, local, *gathered)
    return slab.reshape(tile_count, tile, SLAB_DEV), white, ll.reshape(1)


def solution(mesh):
    placed = (P(None, None, "prow"), P(None, "prow"), P(), P())
    return jax.shard_map(
        shards,
        mesh=mesh,
        in_specs=placed,
        out_specs=(P(None, "prow", "pcol"), P(None, "prow"), P()),
        check_vma=False,
    )
```

```python
import functools
import math

import jax
import jax.numpy as jnp
from jax import lax
from jax.experimental import pallas as pl
from jax.experimental.pallas import tpu as pltpu
from jax.sharding import PartitionSpec as P

SLAB_DEV = 128
NB = 128
SUB = 8


def lane_bcast(v, c):
    return jnp.broadcast_to(v[:, c : c + 1], v.shape)


def row_bcast(v, k):
    return jnp.broadcast_to(v[k : k + 1, :], v.shape)


def split2(x):
    hi = x.astype(jnp.bfloat16)
    lo = (x - hi.astype(jnp.float32)).astype(jnp.bfloat16)
    return hi, lo


def dot_f32(a, b):
    return jnp.dot(a, b, preferred_element_type=jnp.float32)


LOG2E = 1.4426950408889634


def matern(dx, dy, rate):
    d2 = dx * dx + dy * dy
    dist = d2 * lax.rsqrt(jnp.maximum(d2, 1e-30))
    e = jnp.exp2(dist * rate[1])
    return e + (dist * rate[0]) * e


def tree_sum(xs):
    while len(xs) > 1:
        xs = [xs[i] + xs[i + 1] if i + 1 < len(xs) else xs[i] for i in range(0, len(xs), 2)]
    return xs[0]


def factor_block(rows, fill):
    sub = lax.broadcasted_iota(jnp.int32, (SUB, NB), 0)
    lane = lax.broadcasted_iota(jnp.int32, (SUB, NB), 1)
    units = [(sub == k).astype(jnp.float32) for k in range(SUB)]
    groups = len(rows)
    x_all = list(rows)
    out = []
    logs = jnp.zeros((SUB, NB), jnp.float32)
    cols = [lane_bcast(x_all[0], k) for k in range(SUB)]
    d = row_bcast(cols[0], 0)
    for s in range(groups):
        c0 = SUB * s
        more = s + 1 < groups
        if more:
            g_next = [lane_bcast(x_all[s + 1], c0 + k) for k in range(SUB)]
            low = list(g_next)
            ahead = [lane_bcast(x_all[s + 1], c0 + SUB + k) for k in range(SUB)]
        here = (lane >= c0) & (lane < c0 + SUB)
        x = jnp.where(here, (lane == sub + c0).astype(jnp.float32), x_all[s])
        x_out = jnp.zeros((SUB, NB), jnp.float32)
        prod = None
        for k in range(SUB):
            inv = pltpu.reciprocal(d, approx=True)
            rs = lax.rsqrt(d)
            prod = d if prod is None else prod * d
            if k + 1 < SUB:
                e = row_bcast(cols[k + 1], k)
                d = row_bcast(cols[k + 1], k + 1) - (e * e) * inv
            elif more:
                e = row_bcast(low[k], 0)
                d = row_bcast(ahead[0], 0) - (e * e) * inv
            f = cols[k] - units[k]
            fi = f * inv
            h = low[k] * inv if more else None
            for m in range(k + 1, SUB):
                e = row_bcast(cols[m], k)
                cols[m] = cols[m] - ((f * e) * inv if m <= k + 2 else fi * e)
                if more:
                    low[m] = low[m] - h * e
            if more:
                for m in range(SUB):
                    ahead[m] = ahead[m] - h * row_bcast(low[k], m)
            xk = row_bcast(x, k)
            x_out = jnp.where(sub == k, xk * rs, x_out)
            x = x - fi * xk
            fill(s, k)
        logs = logs + jnp.log(prod)
        out.append(jnp.where(lane < c0 + SUB, x_out, 0.0) if more else x_out)
        if more:
            x_rows = [row_bcast(x, k) for k in range(SUB)]
            for t in range(s + 1, groups):
                g = g_next if t == s + 1 else [
                    lane_bcast(x_all[t], c0 + k) for k in range(SUB)
                ]
                x_all[t] = jnp.where(here, 0.0, x_all[t]) - tree_sum(
                    [g[k] * x_rows[k] for k in range(SUB)]
                )
            cols = ahead
    return out, logs


def kernel(
    peers, ls_ref, ng_ref, loc_ref, *refs,
):
    gathered, refs = refs[: peers + 1], refs[peers + 1 :]
    (
        slab_hbm, white_ref, ll_ref, slab_ref, sems, lead_ref, a_ref, z_ref, site_ref, row_ref, chi_ref, clo_ref, p1_ref, p23_ref,
        d_ref, winv_ref, pinv_ref, col_ref, mh_ref, ml_ref,
    ) = refs
    f32, bf16 = jnp.float32, jnp.bfloat16
    tile_count, tile = loc_ref.shape[1:]
    n_lead = 2 * tile
    nblk = n_lead // NB
    width = n_lead + 2 * NB
    rows_total = tile_count * tile
    row_rank = lax.axis_index("prow")
    col_rank = lax.axis_index("pcol")
    row_procs = lax.axis_size("prow")
    if peers:
        for t in range(peers + 1):
            rows = gathered[0][...]
            for m in range(1, peers + 1):
                rows = jnp.where(row_rank == t ^ m, gathered[m][...], rows)
            lead_ref[t] = rows
    else:
        lead_ref[...] = gathered[0][...]
    ls = jnp.full((SUB, NB), ls_ref[0], f32)
    decay = math.sqrt(3.0) / ls
    rate = decay, decay * -LOG2E
    nugget = ng_ref[0]
    col_off = col_rank * SLAB_DEV
    col_tile = 2 + col_off // tile
    col_lane = pl.multiple_of(lax.rem(col_off, tile), SLAB_DEV)
    cx = lead_ref[col_tile, 0:1, pl.ds(col_lane, SLAB_DEV)]
    cy = lead_ref[col_tile, 1:2, pl.ds(col_lane, SLAB_DEV)]
    sub = lax.broadcasted_iota(jnp.int32, (SUB, NB), 0)
    lane = lax.broadcasted_iota(jnp.int32, (SUB, NB), 1)

    def columns(coord):
        pad = jnp.zeros((NB - coord.shape[0], NB), f32)
        return jnp.concatenate([coord, pad], axis=0).T

    def site_columns(q):
        t, o = divmod(q * NB, tile)
        site_ref[q * NB : (q + 1) * NB, :] = columns(lead_ref[t, :, o : o + NB])

    def row_columns(q):
        t, o = divmod(q * NB, tile)
        here = [loc_ref[c, t : t + 1, o : o + NB] for c in range(2)]
        row_ref[q * NB : (q + 1) * NB, :] = columns(jnp.concatenate(here, axis=0))

    held = {}

    def cov_piece(b, g, j):
        o = b * NB + g * SUB
        if ("site", o) not in held:
            v = site_ref[o : o + SUB, :]
            held["site", o] = [lane_bcast(v, c) for c in range(3)]
        x, y, ob = held["site", o]
        if j < nblk:
            t, u = divmod(j * NB, tile)
            val = matern(x - lead_ref[t, 0:1, u : u + NB], y - lead_ref[t, 1:2, u : u + NB], rate)
            if j == b:
                val = jnp.where(lane == sub + g * SUB, val + nugget, val)
        elif j == nblk:
            val = matern(x - cx, y - cy, rate)
        else:
            val = jnp.where(lane < 2, ob, 0.0)
        a_ref[o : o + SUB, j * NB : (j + 1) * NB] = val

    def row_piece(ro, key, j):
        if key not in held:
            held[key] = []
            for h in range(2):
                at = ro + h * SUB
                v = row_ref[pl.ds(at if isinstance(at, int) else pl.multiple_of(at, SUB), SUB), :]
                held[key].append((lane_bcast(v, 0), lane_bcast(v, 1)))
        t, u = divmod(j * NB, tile)
        vals = [
            matern(x - lead_ref[t, 0:1, u : u + NB], y - lead_ref[t, 1:2, u : u + NB], rate)
            for x, y in held[key]
        ]
        hi, lo = split2(jnp.concatenate(vals, axis=0))
        chi_ref[pl.ds(ro, 16), j * NB : (j + 1) * NB] = hi
        clo_ref[pl.ds(ro, 16), j * NB : (j + 1) * NB] = lo

    def three(al_parts, bh, bl):
        return dot_f32(al_parts, jnp.concatenate([bh, bh, bl], axis=0))

    def parts(x):
        h, l = split2(x)
        return jnp.concatenate([h, l, h], axis=1)

    def multiplier_piece(j0, j1):
        m = three(pinv_ref[...], *split2(a_ref[0:NB, j0:j1]))
        mh_ref[:, j0:j1], ml_ref[:, j0:j1] = split2(m)
        return m

    def column_parts():
        col_ref[...] = parts(a_ref[NB:n_lead, 0:NB])

    def update_piece(j0, j1, r0, r1, shift):
        new = a_ref[r0:r1, j0:j1] - three(
            col_ref[r0 - NB : r1 - NB, :], mh_ref[:, j0:j1], ml_ref[:, j0:j1]
        )
        a_ref[r0 - NB : r1 - NB, j0 - shift : j1 - shift] = new

    def tile_pieces(j0, j1, shift):
        box = {}

        def first():
            box["m"] = multiplier_piece(j0, j1)

        def last():
            a_ref[n_lead - NB : n_lead, j0 - shift : j1 - shift] = box["m"]

        half = (nblk // 2 + 1) * NB
        return [
            first,
            functools.partial(update_piece, j0, j1, NB, half, shift),
            functools.partial(update_piece, j0, j1, half, n_lead, shift),
            last,
        ]

    def keep_z(at):
        z_ref[pl.ds(at, NB), :] = three(
            winv_ref[...], *split2(a_ref[0:NB, n_lead + NB : width])
        )

    def finish_block(out, more_blocks):
        w = jnp.concatenate(out, axis=0)
        wt = w.T
        w_parts = parts(w)
        winv_ref[...] = w_parts
        wh, wl = w_parts[:, :NB], w_parts[:, NB : 2 * NB]
        if more_blocks:
            u = three(w_parts, *split2(a_ref[0:NB, NB : 2 * NB]))
            ut = three(parts(a_ref[NB : 2 * NB, 0:NB]), *split2(wt))
            d_ref[...] = a_ref[NB : 2 * NB, NB : 2 * NB] - three(parts(ut), *split2(u))
        pinv_ref[...] = parts(three(parts(wt), wh, wl))

    def load_rows():
        return [d_ref[SUB * t : SUB * (t + 1), :] for t in range(NB // SUB)]

    slots = (NB // SUB) * SUB

    def planned(urgent, work):
        plan = [[] for _ in range(slots)]
        early = slots * 7 // 8
        for i, f in enumerate(urgent):
            plan[i * early // len(urgent)].append(f)
        for i, f in enumerate(work):
            plan[i * slots // len(work)].append(f)

        def fill(s, k):
            for f in plan[s * SUB + k]:
                f()

        return fill

    for q in range(nblk):
        site_columns(q)
    for g in range(NB // SUB):
        cov_piece(0, g, 0)
    d_ref[...] = a_ref[0:NB, 0:NB]
    work = [
        functools.partial(cov_piece, b, g, j)
        for b in range(nblk)
        for g in range(NB // SUB)
        for j in range(nblk + 2)
        if (b, j) != (0, 0)
    ]
    urgent = [functools.partial(row_columns, q) for q in range(rows_total // NB)]
    out, logs = factor_block(load_rows(), planned(urgent, work))
    finish_block(out, True)

    chunk = -(-rows_total // 16 // (nblk - 1)) * 16
    col_tiles = [(j * NB, min(j + 2, nblk) * NB) for j in range(1, nblk, 2)]

    def step(b, logs):
        held.clear()
        base = jnp.minimum((b - 1) * chunk, rows_total - chunk)
        work = [
            functools.partial(
                row_piece, pl.multiple_of(base + pair * 16, 16), ("row", pair), j
            )
            for pair in range(chunk // 16)
            for j in range(nblk)
        ]
        urgent = [column_parts]
        for j0, j1 in col_tiles:
            urgent += tile_pieces(j0, j1, NB)
        urgent += [functools.partial(keep_z, pl.multiple_of((b - 1) * NB, NB))]
        urgent += tile_pieces(n_lead, width, 0)
        out, more = factor_block(load_rows(), planned(urgent, work))
        finish_block(out, True)
        return logs + more

    logs = lax.fori_loop(1, nblk, step, logs)
    column_parts()
    keep_z(n_lead - NB)
    for f in tile_pieces(n_lead, width, 0):
        f()

    y = a_ref[:, n_lead:width]
    yh, yl = split2(y)
    yt = ((y - yh.astype(f32)) - yl.astype(f32)).astype(bf16)
    first = lax.broadcasted_iota(jnp.int32, (n_lead, NB), 1) == 0
    p1_ref[...] = jnp.concatenate([yh[:, :NB], yl[:, :NB]], axis=1)
    obs_h, obs_l = yh[:, NB:].astype(f32), yl[:, NB:].astype(f32)
    p23_ref[0:n_lead, :] = jnp.concatenate(
        [yt[:, :NB], jnp.where(first, obs_h, obs_l).astype(bf16)], axis=1
    )
    p23_ref[n_lead : 2 * n_lead, :] = jnp.concatenate(
        [yh[:, :NB], jnp.where(first, obs_h, 0.0).astype(bf16)], axis=1
    )

    z = z_ref[...]
    quad = 0.5 * jnp.sum(jnp.where(first, z * z, 0.0), keepdims=True)
    ll_ref[...] = -(quad + 0.5 * logs[0:1, 0:1]) / float(n_lead)

    def slab_copy(t):
        o = pl.multiple_of(t * tile, tile)
        return pltpu.make_async_copy(
            slab_ref.at[pl.ds(o, tile)], slab_hbm.at[pl.ds(o, tile)], sems.at[t]
        )

    tile_row = lax.broadcasted_iota(jnp.int32, (tile_count, NB), 0)

    def finish(t, carry):
        o = pl.multiple_of(t * tile, tile)
        ch = chi_ref[pl.ds(o, tile), :]
        acc = dot_f32(ch, p1_ref[...])
        acc2 = dot_f32(jnp.concatenate([ch, clo_ref[pl.ds(o, tile), :]], axis=1), p23_ref[...])
        corr = acc[:, :NB] + (acc[:, NB:] + acc2[:, :NB])
        gid = (t * row_procs + row_rank) * tile
        leading = gid < n_lead
        v = row_ref[pl.ds(o, tile), :]
        x = jnp.broadcast_to(v[:, 0:1], (tile, NB))
        y = jnp.broadcast_to(v[:, 1:2], (tile, NB))
        val = matern(x - cx, y - cy, (rate[0][0:1, :], rate[1][0:1, :]))
        rid = gid + lax.broadcasted_iota(jnp.int32, (tile, NB), 0)
        cid = n_lead + col_off + lax.broadcasted_iota(jnp.int32, (tile, NB), 1)
        val = jnp.where(rid == cid, val + nugget, val) - corr
        slab_ref[pl.ds(o, tile), :] = jnp.where(leading, 0.0, val)
        slab_copy(t).start()
        for h in range(tile // NB):
            at = h * NB
            tr = acc2[at : at + NB, NB:].T
            rest = loc_ref[2, :, at : at + NB] - (tr[0:1, :] + tr[1:2, :])
            zs = pl.multiple_of(jnp.where(leading, gid, 0) + at, NB)
            zt = z_ref[pl.ds(zs, NB), :].T
            rest = jnp.where(leading, zt[0:1, :], rest)
            kept = white_ref[:, at : at + NB]
            white_ref[:, at : at + NB] = jnp.where(tile_row == t, rest, kept)
        return carry

    lax.fori_loop(0, tile_count, finish, 0)
    for t in range(tile_count):
        slab_copy(t).wait()


def shards(coords, observations, length_scale, nugget):
    tile_count, tile = coords.shape[1:]
    rows = tile_count * tile
    n_lead = 2 * tile
    width = n_lead + 2 * NB
    f32, bf16 = jnp.float32, jnp.bfloat16
    procs = lax.axis_size("prow")
    local = lax.optimization_barrier(jnp.concatenate([coords, observations[None]], axis=0))
    mine = local[:, 0, :]
    if procs <= 4 and procs & (procs - 1) == 0:
        peers = procs - 1
        gathered = [mine] + [
            lax.ppermute(mine, "prow", [(r, r ^ m) for r in range(procs)])
            for m in range(1, procs)
        ]
    else:
        peers = 0
        gathered = [lax.all_gather(mine, "prow", axis=0)]
    vmem = pl.BlockSpec(memory_space=pltpu.VMEM)
    smem = pl.BlockSpec(memory_space=pltpu.SMEM)
    slab, white, ll = pl.pallas_call(
        functools.partial(kernel, peers),
        out_shape=(
            jax.ShapeDtypeStruct((rows, SLAB_DEV), f32),
            jax.ShapeDtypeStruct((tile_count, tile), f32),
            jax.ShapeDtypeStruct((1, 1), f32),
        ),
        in_specs=[smem, smem, vmem] + [vmem] * len(gathered),
        out_specs=(pl.BlockSpec(memory_space=pl.ANY), vmem, vmem),
        scratch_shapes=[
            pltpu.VMEM((rows, SLAB_DEV), f32),
            pltpu.SemaphoreType.DMA((tile_count,)),
            pltpu.VMEM((procs, 3, tile), f32),
            pltpu.VMEM((n_lead, width), f32),
            pltpu.VMEM((n_lead, NB), f32),
            pltpu.VMEM((n_lead, NB), f32),
            pltpu.VMEM((rows, NB), f32),
            pltpu.VMEM((rows, n_lead), bf16),
            pltpu.VMEM((rows, n_lead), bf16),
            pltpu.VMEM((n_lead, 2 * NB), bf16),
            pltpu.VMEM((2 * n_lead, 2 * NB), bf16),
            pltpu.VMEM((NB, NB), f32),
            pltpu.VMEM((NB, 3 * NB), bf16),
            pltpu.VMEM((NB, 3 * NB), bf16),
            pltpu.VMEM((n_lead - NB, 3 * NB), bf16),
            pltpu.VMEM((NB, width), bf16),
            pltpu.VMEM((NB, width), bf16),
        ],
        compiler_params=pltpu.CompilerParams(vmem_limit_bytes=48 * 1024 * 1024),
    )(length_scale, nugget, local, *gathered)
    return slab.reshape(tile_count, tile, SLAB_DEV), white, ll.reshape(1)


def solution(mesh):
    placed = (P(None, None, "prow"), P(None, "prow"), P(), P())
    return jax.shard_map(
        shards,
        mesh=mesh,
        in_specs=placed,
        out_specs=(P(None, "prow", "pcol"), P(None, "prow"), P()),
        check_vma=False,
    )
```

```python
import functools

import jax
import jax.numpy as jnp
from jax import lax
from jax.experimental import pallas as pl
from jax.experimental.pallas import tpu as pltpu
from jax.sharding import PartitionSpec as P

SLAB_DEV = 128
NB = 128
SUB = 8


def lane_bcast(v, c):
    return jnp.broadcast_to(v[:, c : c + 1], v.shape)


def row_bcast(v, k):
    return jnp.broadcast_to(v[k : k + 1, :], v.shape)


def split2(x):
    hi = x.astype(jnp.bfloat16)
    lo = (x - hi.astype(jnp.float32)).astype(jnp.bfloat16)
    return hi, lo


def dot_f32(a, b):
    return jnp.dot(a, b, preferred_element_type=jnp.float32)


LOG2E = 1.4426950408889634


def matern(dx, dy, rate2):
    t = (dx * dx + dy * dy) * rate2
    s = t * lax.rsqrt(jnp.maximum(t, 1e-30))
    e = jnp.exp2(s * -LOG2E)
    return e + s * e


def tree_sum(xs):
    while len(xs) > 1:
        xs = [xs[i] + xs[i + 1] if i + 1 < len(xs) else xs[i] for i in range(0, len(xs), 2)]
    return xs[0]


def factor_block(rows, fill):
    sub = lax.broadcasted_iota(jnp.int32, (SUB, NB), 0)
    lane = lax.broadcasted_iota(jnp.int32, (SUB, NB), 1)
    units = [(sub == k).astype(jnp.float32) for k in range(SUB)]
    groups = len(rows)
    x_all = list(rows)
    out = []
    logs = jnp.zeros((SUB, NB), jnp.float32)
    cols = [lane_bcast(x_all[0], k) for k in range(SUB)]
    d = row_bcast(cols[0], 0)
    for s in range(groups):
        c0 = SUB * s
        more = s + 1 < groups
        if more:
            low = [lane_bcast(x_all[s + 1], c0 + k) for k in range(SUB)]
            ahead = [lane_bcast(x_all[s + 1], c0 + SUB + k) for k in range(SUB)]
        here = (lane >= c0) & (lane < c0 + SUB)
        near = range(s + 1, min(s + 3, groups))
        lows = [list(low)] if more else []
        if s + 2 < groups:
            lows.append([lane_bcast(x_all[s + 2], c0 + k) for k in range(SUB)])
        x_near = [jnp.where(here, 0.0, x_all[t]) for t in near]
        x = jnp.where(here, (lane == sub + c0).astype(jnp.float32), x_all[s])
        x_out = jnp.zeros((SUB, NB), jnp.float32)
        prod = None
        for k in range(SUB):
            inv = pltpu.reciprocal(d, approx=True)
            rs = lax.rsqrt(d)
            prod = d if prod is None else prod * d
            if k + 1 < SUB:
                e = row_bcast(cols[k + 1], k)
                d = row_bcast(cols[k + 1], k + 1) - (e * e) * inv
            elif more:
                e = row_bcast(lows[0][k], 0)
                d = row_bcast(ahead[0], 0) - (e * e) * inv
            f = cols[k] - units[k]
            fi = f * inv
            hs = [low[k] * inv for low in lows]
            for m in range(k + 1, SUB):
                e = row_bcast(cols[m], k)
                cols[m] = cols[m] - ((f * e) * inv if m <= k + 2 else fi * e)
                for low, h in zip(lows, hs):
                    low[m] = low[m] - h * e
            if more:
                for m in range(SUB):
                    ahead[m] = ahead[m] - hs[0] * row_bcast(lows[0][k], m)
            xk = row_bcast(x, k)
            x_near = [v - h * xk for v, h in zip(x_near, hs)]
            x_out = jnp.where(sub == k, xk * rs, x_out)
            x = x - fi * xk
            fill(s, k)
        logs = logs + jnp.log(prod)
        out.append(jnp.where(lane < c0 + SUB, x_out, 0.0) if more else x_out)
        if more:
            x_rows = [row_bcast(x, k) for k in range(SUB)]
            for t, v in zip(near, x_near):
                x_all[t] = v
            for t in range(s + 3, groups):
                g = [lane_bcast(x_all[t], c0 + k) for k in range(SUB)]
                x_all[t] = jnp.where(here, 0.0, x_all[t]) - tree_sum(
                    [g[k] * x_rows[k] for k in range(SUB)]
                )
            cols = ahead
    return out, logs


def kernel(
    peers, ls_ref, ng_ref, loc_ref, *refs,
):
    gathered, refs = refs[: peers + 1], refs[peers + 1 :]
    (
        slab_ref, white_ref, ll_ref, lead_ref, a_ref, z_ref, site_ref, row_ref, chi_ref, clo_ref, p1_ref, p23_ref,
        d_ref, winv_ref, pinv_ref, col_ref, mh_ref, ml_ref,
    ) = refs
    f32, bf16 = jnp.float32, jnp.bfloat16
    tile_count, tile = loc_ref.shape[1:]
    n_lead = 2 * tile
    nblk = n_lead // NB
    width = n_lead + 2 * NB
    rows_total = tile_count * tile
    row_rank = lax.axis_index("prow")
    col_rank = lax.axis_index("pcol")
    row_procs = lax.axis_size("prow")
    if peers:
        for t in range(peers + 1):
            rows = gathered[0][...]
            for m in range(1, peers + 1):
                rows = jnp.where(row_rank == t ^ m, gathered[m][...], rows)
            lead_ref[t] = rows
    else:
        lead_ref[...] = gathered[0][...]
    ls = jnp.full((SUB, NB), ls_ref[0], f32)
    rate2 = 3.0 / (ls * ls)
    nugget = ng_ref[0]
    col_off = col_rank * SLAB_DEV
    col_tile = 2 + col_off // tile
    col_lane = pl.multiple_of(lax.rem(col_off, tile), SLAB_DEV)
    cx = lead_ref[col_tile, 0:1, pl.ds(col_lane, SLAB_DEV)]
    cy = lead_ref[col_tile, 1:2, pl.ds(col_lane, SLAB_DEV)]
    sub = lax.broadcasted_iota(jnp.int32, (SUB, NB), 0)
    lane = lax.broadcasted_iota(jnp.int32, (SUB, NB), 1)

    def columns(coord):
        pad = jnp.zeros((NB - coord.shape[0], NB), f32)
        return jnp.concatenate([coord, pad], axis=0).T

    def site_columns(q):
        t, o = divmod(q * NB, tile)
        site_ref[q * NB : (q + 1) * NB, :] = columns(lead_ref[t, :, o : o + NB])

    def row_columns(q):
        t, o = divmod(q * NB, tile)
        here = [loc_ref[c, t : t + 1, o : o + NB] for c in range(2)]
        row_ref[q * NB : (q + 1) * NB, :] = columns(jnp.concatenate(here, axis=0))

    held = {}

    def cov_piece(b, g, j):
        o = b * NB + g * SUB
        if ("site", o) not in held:
            v = site_ref[o : o + SUB, :]
            held["site", o] = [lane_bcast(v, c) for c in range(3)]
        x, y, ob = held["site", o]
        if j < nblk:
            t, u = divmod(j * NB, tile)
            val = matern(x - lead_ref[t, 0:1, u : u + NB], y - lead_ref[t, 1:2, u : u + NB], rate2)
            if j == b:
                val = jnp.where(lane == sub + g * SUB, val + nugget, val)
        elif j == nblk:
            val = matern(x - cx, y - cy, rate2)
        else:
            val = jnp.where(lane < 2, ob, 0.0)
        a_ref[o : o + SUB, j * NB : (j + 1) * NB] = val

    def row_piece(ro, key, j):
        if key not in held:
            held[key] = []
            for h in range(2):
                at = ro + h * SUB
                v = row_ref[pl.ds(at if isinstance(at, int) else pl.multiple_of(at, SUB), SUB), :]
                held[key].append((lane_bcast(v, 0), lane_bcast(v, 1)))
        t, u = divmod(j * NB, tile)
        vals = [
            matern(x - lead_ref[t, 0:1, u : u + NB], y - lead_ref[t, 1:2, u : u + NB], rate2)
            for x, y in held[key]
        ]
        hi, lo = split2(jnp.concatenate(vals, axis=0))
        chi_ref[pl.ds(ro, 16), j * NB : (j + 1) * NB] = hi
        clo_ref[pl.ds(ro, 16), j * NB : (j + 1) * NB] = lo

    def three(al_parts, bh, bl):
        return dot_f32(al_parts, jnp.concatenate([bh, bh, bl], axis=0))

    def parts(x):
        h, l = split2(x)
        return jnp.concatenate([h, l, h], axis=1)

    def multiplier_piece(j0, j1):
        m = three(pinv_ref[...], *split2(a_ref[0:NB, j0:j1]))
        mh_ref[:, j0:j1], ml_ref[:, j0:j1] = split2(m)
        return m

    def column_parts():
        col_ref[...] = parts(a_ref[NB:n_lead, 0:NB])

    def update_piece(j0, j1, r0, r1, shift):
        new = a_ref[r0:r1, j0:j1] - three(
            col_ref[r0 - NB : r1 - NB, :], mh_ref[:, j0:j1], ml_ref[:, j0:j1]
        )
        a_ref[r0 - NB : r1 - NB, j0 - shift : j1 - shift] = new

    def tile_pieces(j0, j1, shift):
        box = {}

        def first():
            box["m"] = multiplier_piece(j0, j1)

        def last():
            a_ref[n_lead - NB : n_lead, j0 - shift : j1 - shift] = box["m"]

        half = (nblk // 2 + 1) * NB
        return [
            first,
            functools.partial(update_piece, j0, j1, NB, half, shift),
            functools.partial(update_piece, j0, j1, half, n_lead, shift),
            last,
        ]

    def keep_z(at):
        z_ref[pl.ds(at, NB), :] = three(
            winv_ref[...], *split2(a_ref[0:NB, n_lead + NB : width])
        )

    def finish_block(out, more_blocks):
        w = jnp.concatenate(out, axis=0)
        wt = w.T
        w_parts = parts(w)
        winv_ref[...] = w_parts
        wh, wl = w_parts[:, :NB], w_parts[:, NB : 2 * NB]
        if more_blocks:
            u = three(w_parts, *split2(a_ref[0:NB, NB : 2 * NB]))
            ut = three(parts(a_ref[NB : 2 * NB, 0:NB]), *split2(wt))
            d_ref[...] = a_ref[NB : 2 * NB, NB : 2 * NB] - three(parts(ut), *split2(u))
        pinv_ref[...] = parts(three(parts(wt), wh, wl))

    def load_rows():
        return [d_ref[SUB * t : SUB * (t + 1), :] for t in range(NB // SUB)]

    slots = (NB // SUB) * SUB

    def planned(urgent, work):
        plan = [[] for _ in range(slots)]
        early = slots * 7 // 8
        for i, f in enumerate(urgent):
            plan[i * early // len(urgent)].append(f)
        for i, f in enumerate(work):
            plan[i * slots // len(work)].append(f)

        def fill(s, k):
            for f in plan[s * SUB + k]:
                f()

        return fill

    for q in range(nblk):
        site_columns(q)
    for g in range(NB // SUB):
        cov_piece(0, g, 0)
    d_ref[...] = a_ref[0:NB, 0:NB]
    work = [
        functools.partial(cov_piece, b, g, j)
        for b in range(nblk)
        for g in range(NB // SUB)
        for j in range(nblk + 2)
        if (b, j) != (0, 0)
    ]
    urgent = [functools.partial(row_columns, q) for q in range(rows_total // NB)]
    out, logs = factor_block(load_rows(), planned(urgent, work))
    finish_block(out, True)

    big = 2 * NB
    early_rows = rows_total * 3 // 4 // big * big
    chunk = -(-early_rows // 16 // (nblk - 1)) * 16
    col_tiles = [(j * NB, min(j + 2, nblk) * NB) for j in range(1, nblk, 2)]

    def step(b, logs):
        held.clear()
        base = jnp.minimum((b - 1) * chunk, early_rows - chunk)
        work = [
            functools.partial(
                row_piece, pl.multiple_of(base + pair * 16, 16), ("row", pair), j
            )
            for pair in range(chunk // 16)
            for j in range(nblk)
        ]
        urgent = [column_parts]
        for j0, j1 in col_tiles:
            urgent += tile_pieces(j0, j1, NB)
        urgent += [functools.partial(keep_z, pl.multiple_of((b - 1) * NB, NB))]
        urgent += tile_pieces(n_lead, width, 0)
        out, more = factor_block(load_rows(), planned(urgent, work))
        finish_block(out, True)
        return logs + more

    logs = lax.fori_loop(1, nblk, step, logs)
    column_parts()
    keep_z(n_lead - NB)
    for f in tile_pieces(n_lead, width, 0):
        f()

    y = a_ref[:, n_lead:width]
    yh, yl = split2(y)
    yt = ((y - yh.astype(f32)) - yl.astype(f32)).astype(bf16)
    first = lax.broadcasted_iota(jnp.int32, (n_lead, NB), 1) == 0
    p1_ref[...] = jnp.concatenate([yh[:, :NB], yl[:, :NB]], axis=1)
    obs_h, obs_l = yh[:, NB:].astype(f32), yl[:, NB:].astype(f32)
    p23_ref[0:n_lead, :] = jnp.concatenate(
        [yt[:, :NB], jnp.where(first, obs_h, obs_l).astype(bf16)], axis=1
    )
    p23_ref[n_lead : 2 * n_lead, :] = jnp.concatenate(
        [yh[:, :NB], jnp.where(first, obs_h, 0.0).astype(bf16)], axis=1
    )

    z = z_ref[...]
    quad = 0.5 * jnp.sum(jnp.where(first, z * z, 0.0), keepdims=True)
    ll_ref[...] = -(quad + 0.5 * logs[0:1, 0:1]) / float(n_lead)

    held.clear()
    late = [
        functools.partial(row_piece, ro, ("late", ro), j)
        for ro in range(early_rows, rows_total, 16)
        for j in range(nblk)
    ]
    turns = early_rows // big
    for q in range(rows_total // big):
        o = q * big
        for f in late[len(late) * q // turns : len(late) * (q + 1) // turns]:
            f()
        ch = chi_ref[o : o + big, :]
        acc = dot_f32(ch, p1_ref[...])
        acc2 = dot_f32(jnp.concatenate([ch, clo_ref[o : o + big, :]], axis=1), p23_ref[...])
        corr = acc[:, :NB] + (acc[:, NB:] + acc2[:, :NB])
        t, off = divmod(o, tile)
        gid = (t * row_procs + row_rank) * tile + off
        leading = gid < n_lead
        v = row_ref[o : o + big, :]
        x = jnp.broadcast_to(v[:, 0:1], (big, NB))
        y = jnp.broadcast_to(v[:, 1:2], (big, NB))
        val = matern(x - cx, y - cy, rate2[0:1, :])
        rid = gid + lax.broadcasted_iota(jnp.int32, (big, NB), 0)
        cid = n_lead + col_off + lax.broadcasted_iota(jnp.int32, (big, NB), 1)
        val = jnp.where(rid == cid, val + nugget, val) - corr
        slab_ref[o : o + big, :] = jnp.where(leading, 0.0, val)
        for h in range(big // NB):
            at = off + h * NB
            tr = acc2[h * NB : (h + 1) * NB, NB:].T
            rest = loc_ref[2, t : t + 1, at : at + NB] - (tr[0:1, :] + tr[1:2, :])
            if t == 0:
                zs = pl.multiple_of(jnp.where(leading, gid, 0) + h * NB, NB)
                zt = z_ref[pl.ds(zs, NB), :].T
                rest = jnp.where(leading, zt[0:1, :], rest)
            white_ref[t : t + 1, at : at + NB] = rest


def shards(coords, observations, length_scale, nugget):
    tile_count, tile = coords.shape[1:]
    rows = tile_count * tile
    n_lead = 2 * tile
    width = n_lead + 2 * NB
    f32, bf16 = jnp.float32, jnp.bfloat16
    procs = lax.axis_size("prow")
    local = lax.optimization_barrier(jnp.concatenate([coords, observations[None]], axis=0))
    mine = local[:, 0, :]
    if procs <= 4 and procs & (procs - 1) == 0:
        peers = procs - 1
        gathered = [mine] + [
            lax.ppermute(mine, "prow", [(r, r ^ m) for r in range(procs)])
            for m in range(1, procs)
        ]
    else:
        peers = 0
        gathered = [lax.all_gather(mine, "prow", axis=0)]
    vmem = pl.BlockSpec(memory_space=pltpu.VMEM)
    smem = pl.BlockSpec(memory_space=pltpu.SMEM)
    slab, white, ll = pl.pallas_call(
        functools.partial(kernel, peers),
        out_shape=(
            jax.ShapeDtypeStruct((rows, SLAB_DEV), f32),
            jax.ShapeDtypeStruct((tile_count, tile), f32),
            jax.ShapeDtypeStruct((1, 1), f32),
        ),
        in_specs=[smem, smem, vmem] + [vmem] * len(gathered),
        out_specs=(vmem, vmem, vmem),
        scratch_shapes=[
            pltpu.VMEM((procs, 3, tile), f32),
            pltpu.VMEM((n_lead, width), f32),
            pltpu.VMEM((n_lead, NB), f32),
            pltpu.VMEM((n_lead, NB), f32),
            pltpu.VMEM((rows, NB), f32),
            pltpu.VMEM((rows, n_lead), bf16),
            pltpu.VMEM((rows, n_lead), bf16),
            pltpu.VMEM((n_lead, 2 * NB), bf16),
            pltpu.VMEM((2 * n_lead, 2 * NB), bf16),
            pltpu.VMEM((NB, NB), f32),
            pltpu.VMEM((NB, 3 * NB), bf16),
            pltpu.VMEM((NB, 3 * NB), bf16),
            pltpu.VMEM((n_lead - NB, 3 * NB), bf16),
            pltpu.VMEM((NB, width), bf16),
            pltpu.VMEM((NB, width), bf16),
        ],
        compiler_params=pltpu.CompilerParams(vmem_limit_bytes=48 * 1024 * 1024),
    )(length_scale, nugget, local, *gathered)
    return slab.reshape(tile_count, tile, SLAB_DEV), white, ll.reshape(1)


def solution(mesh):
    placed = (P(None, None, "prow"), P(None, "prow"), P(), P())
    return jax.shard_map(
        shards,
        mesh=mesh,
        in_specs=placed,
        out_specs=(P(None, "prow", "pcol"), P(None, "prow"), P()),
        check_vma=False,
    )
```
